32 devices in a mesh: row: 32 (over z, y, x, core), col: 1.
Axes of the slice: x: 2, y: 2, z: 4, core: 2. Of those that a mesh axis runs over, the one named last changes fastest.
Arguments:
- homolog_features: bfloat16 [64, 128, 256], P(None, ('col', 'row')), may hold values from -6 to 6
- standardize_multiplier: float32 [256], replicated, may hold values from 0.1 to 1.9
- first_factor_weights: bfloat16 [256, 32], replicated, may hold values from -0.375 to 0.375
- second_factor_weights: bfloat16 [256, 32], replicated, may hold values from -0.375 to 0.375
- output_projection_matrix: bfloat16 [1024, 128], replicated, may hold values from -1.5 to 1.5
- output_bias: float32 [128], replicated, may hold values from -3 to 3
- pair_cotangent: bfloat16 [128, 128, 128], P('row', 'col'), may hold values from -2 to 2
Outputs:
- pair_delta: bfloat16 [128, 128, 128], P('row', 'col')
- alignment_gradient: bfloat16 [64, 128, 256], P(None, ('col', 'row'))
- gain_gradient: float32 [256], replicated
- left_projection_gradient: float32 [256, 32], replicated
- right_projection_gradient: float32 [256, 32], replicated
- output_projection_gradient: float32 [1024, 128], P(('row', 'col'))
- output_bias_gradient: float32 [128], replicated
The draws below stay inside these ranges and needn't reach their ends.
All inputs are finite; a program needn't handle non-finite values.
Results may differ from the reference program's by a relative error of at most 0.0072.
Values may be sent and summed in bfloat16 or wider, within the bound.
No kernel may reach another device: no remote copies, remote signals or barrier semaphores. Data moves between devices by JAX's collectives and lax.ppermute only.
A program may use at most 64 MiB of HBM per device.

```python
import jax
import jax.numpy as jnp
from jax import lax

FEATURE_DIMS = 256
HIDDEN_WIDTH = 32
COUPLING_DIMS = 128
HOMOLOG_TOTAL = 64
WINDOW_AMINOS = 128


def levels(own_key, shape, cuts, least, high):
    factor_of, own = 1.0, jax.random.fold_in(own_key, 6)
    for axis_at, shards_of in cuts:
        draws = jnp.exp(jax.random.uniform(jax.random.fold_in(own, axis_at), (shards_of,), jnp.float32, least / len(cuts), high / len(cuts)))
        factor_of = factor_of * jnp.repeat(draws, shape[axis_at] // shards_of).reshape([-1 if axis == axis_at else 1 for axis in range(len(shape))])
    return factor_of


def normal_values(key, dims, width, most, shards=(), held_as=jnp.bfloat16):
    values = jax.random.normal(key, dims, jnp.float32) * width
    if len(shards) > 0:
        values = levels(key, dims, shards, -0.22, 0.18) * values
    return jnp.clip(values, min=-most, max=most).astype(held_as)


def setup_inputs(seed: int = 0) -> dict:
    seeds = jax.random.split(jax.random.key(seed), 8)
    homolog_features = normal_values(seeds[0], (HOMOLOG_TOTAL, WINDOW_AMINOS, FEATURE_DIMS), 1.0, 6.0, ((1, 32),))
    standardize_multiplier = jnp.clip(1.0 + 0.18 * jax.random.normal(seeds[1], (FEATURE_DIMS,), jnp.float32), 0.1, 1.9)
    first_factor_weights = normal_values(seeds[2], (FEATURE_DIMS, HIDDEN_WIDTH), FEATURE_DIMS ** -0.5, 0.375)
    second_factor_weights = normal_values(seeds[3], (FEATURE_DIMS, HIDDEN_WIDTH), FEATURE_DIMS ** -0.5, 0.375)
    output_projection_matrix = normal_values(seeds[4], (HIDDEN_WIDTH * HIDDEN_WIDTH, COUPLING_DIMS), 0.25, 1.5)
    output_bias = normal_values(seeds[5], (COUPLING_DIMS,), 0.5, 3.0, (), jnp.float32)
    pair_cotangent = normal_values(seeds[6], (WINDOW_AMINOS, WINDOW_AMINOS, COUPLING_DIMS), 0.3, 2.0, ((0, 32),))
    return {"homolog_features": homolog_features, "standardize_multiplier": standardize_multiplier, "first_factor_weights": first_factor_weights, "second_factor_weights": second_factor_weights, "output_projection_matrix": output_projection_matrix, "output_bias": output_bias, "pair_cotangent": pair_cotangent}


ln_epsilon = 1e-05

def layer_norm_output(homolog_features, standardize_multiplier):
    value_entries = homolog_features.astype(jnp.float32)
    centred = value_entries - lax.optimization_barrier(jnp.mean(value_entries, axis=-1, keepdims=True))
    reciprocal_deviation = lax.rsqrt(lax.optimization_barrier(jnp.mean(centred * centred, axis=-1, keepdims=True)) + ln_epsilon)
    scaled_rows = centred * reciprocal_deviation
    normalized_rows = (scaled_rows * standardize_multiplier).astype(jnp.bfloat16)
    return (scaled_rows, reciprocal_deviation, normalized_rows)

def reference(homolog_features, standardize_multiplier, first_factor_weights, second_factor_weights, output_projection_matrix, output_bias, pair_cotangent):
    scaled_rows, reciprocal_deviation, normalized_rows = layer_norm_output(homolog_features, standardize_multiplier)
    left = jnp.dot(normalized_rows, first_factor_weights, preferred_element_type=jnp.float32).astype(jnp.bfloat16)
    right = jnp.dot(normalized_rows, second_factor_weights, preferred_element_type=jnp.float32).astype(jnp.bfloat16)
    amino_positions = left.shape[1]
    group = 4
    blocks = amino_positions // group
    right_wide = right.astype(jnp.float32)
    per_homolog_weight = 1.0 / HOMOLOG_TOTAL

    def pair_step(carried, index_val):
        out_acc, right_acc = carried
        offset_row = (index_val * group).astype(jnp.int32)
        left_blk = lax.dynamic_slice_in_dim(left, offset_row, group, 1).astype(jnp.float32)
        grad_blk = lax.dynamic_slice_in_dim(pair_cotangent, offset_row, group, 0)
        outer = jnp.einsum('sic,sjd->ijcd', left_blk, right_wide) * per_homolog_weight
        outer_bf = outer.reshape(group * amino_positions, HIDDEN_WIDTH * HIDDEN_WIDTH).astype(jnp.bfloat16)
        update = (jnp.dot(outer_bf, output_projection_matrix, preferred_element_type=jnp.float32) + output_bias).astype(jnp.bfloat16)
        grad_rows = grad_blk.reshape(group * amino_positions, COUPLING_DIMS)
        out_acc = out_acc + jnp.dot(outer_bf.T, grad_rows, preferred_element_type=jnp.float32)
        outer_grad = jnp.dot(grad_rows, output_projection_matrix.T, preferred_element_type=jnp.float32).astype(jnp.bfloat16)
        outer_grad = outer_grad.reshape(group, amino_positions, HIDDEN_WIDTH, HIDDEN_WIDTH).astype(jnp.float32)
        left_blk_grad = jnp.einsum('ijcd,sjd->sic', outer_grad, right_wide) * per_homolog_weight
        right_acc = right_acc + jnp.einsum('ijcd,sic->sjd', outer_grad, left_blk) * per_homolog_weight
        return ((out_acc, right_acc), (update.reshape(group, amino_positions, COUPLING_DIMS), left_blk_grad))
    initial_carry = (jnp.zeros((HIDDEN_WIDTH * HIDDEN_WIDTH, COUPLING_DIMS), jnp.float32), jnp.zeros((HOMOLOG_TOTAL, amino_positions, HIDDEN_WIDTH), jnp.float32))
    (out_acc, right_sum), (updates, first_factor_pieces) = lax.scan(pair_step, initial_carry, jnp.arange(blocks, dtype=jnp.int32))
    pair_delta = updates.reshape(amino_positions, amino_positions, COUPLING_DIMS)
    first_factor_total = jnp.transpose(first_factor_pieces, (1, 0, 2, 3)).reshape(HOMOLOG_TOTAL, amino_positions, HIDDEN_WIDTH)
    left_bf = first_factor_total.astype(jnp.bfloat16)
    right_bf = right_sum.astype(jnp.bfloat16)
    normed_grad = jnp.dot(left_bf, first_factor_weights.T, preferred_element_type=jnp.float32) + jnp.dot(right_bf, second_factor_weights.T, preferred_element_type=jnp.float32)
    scaled_gradient = normed_grad * standardize_multiplier
    centering_term = lax.optimization_barrier(jnp.mean(scaled_gradient, axis=-1, keepdims=True))
    gradient_slope_term = lax.optimization_barrier(jnp.mean(scaled_gradient * scaled_rows, axis=-1, keepdims=True))
    alignment_gradient = (reciprocal_deviation * (scaled_gradient - centering_term - scaled_rows * gradient_slope_term)).astype(jnp.bfloat16)
    scale = 1.0 / WINDOW_AMINOS
    gain_gradient = lax.optimization_barrier(jnp.sum(normed_grad * scaled_rows, axis=(0, 1))) * scale
    normed_wide = normalized_rows.astype(jnp.float32)
    left_projection_gradient = jnp.einsum('srm,srh->mh', normed_wide, left_bf.astype(jnp.float32)) * scale
    right_projection_gradient = jnp.einsum('srm,srh->mh', normed_wide, right_bf.astype(jnp.float32)) * scale
    output_projection_gradient = out_acc * scale
    output_bias_gradient = lax.optimization_barrier(jnp.sum(pair_cotangent.astype(jnp.float32), axis=(0, 1))) * scale
    return (pair_delta, alignment_gradient, gain_gradient, left_projection_gradient, right_projection_gradient, output_projection_gradient, output_bias_gradient)
```

```python
import math

import jax
import jax.numpy as jnp
from jax import lax
from jax.experimental import pallas as pl
from jax.experimental.pallas import tpu as pltpu
from jax.sharding import PartitionSpec as P

ln_epsilon = 1e-05


def from_root(value, axis, root):
    mine = lax.axis_index(axis) == root
    return lax.psum(jnp.where(mine, value, jnp.zeros_like(value)), axis)


def layer_norm_output(homolog_features, standardize_multiplier):
    value_entries = homolog_features.astype(jnp.float32)
    centred = value_entries - jnp.mean(value_entries, axis=-1, keepdims=True)
    reciprocal_deviation = lax.rsqrt(
        jnp.mean(centred * centred, axis=-1, keepdims=True) + ln_epsilon
    )
    scaled_rows = centred * reciprocal_deviation
    normalized_rows = (scaled_rows * standardize_multiplier).astype(jnp.bfloat16)
    return (scaled_rows, reciprocal_deviation, normalized_rows)


def on_device(
    homolog_features,
    standardize_multiplier,
    first_factor_weights,
    second_factor_weights,
    output_projection_matrix,
    output_bias,
    pair_cotangent,
):
    sequence_count, local_residues, channel_count = homolog_features.shape
    hidden = first_factor_weights.shape[1]
    pair_channels = output_projection_matrix.shape[1]
    row_count = lax.axis_size("row")
    col_count = lax.axis_size("col")
    ratio = row_count // col_count
    row_index = lax.axis_index("row")
    col_index = lax.axis_index("col")
    scaled_rows, reciprocal_deviation, normalized_rows = layer_norm_output(
        homolog_features, standardize_multiplier
    )
    left_own = jnp.dot(
        normalized_rows, first_factor_weights, preferred_element_type=jnp.float32
    ).astype(jnp.bfloat16)
    right_own = jnp.dot(
        normalized_rows, second_factor_weights, preferred_element_type=jnp.float32
    ).astype(jnp.bfloat16)
    left_cols, right_cols = (
        lax.all_gather(
            left_own.reshape(sequence_count, local_residues * hidden), "row", axis=1, tiled=True
        ),
        lax.all_gather(
            right_own.reshape(sequence_count, local_residues * hidden), "row", axis=1, tiled=True
        ),
    )
    col_res = local_residues * row_count
    row_res = col_res // ratio
    offset = row_index % ratio * row_res
    piece_flat = lax.dynamic_slice_in_dim(left_cols, offset * hidden, row_res * hidden, 1)
    left_rows = from_root(piece_flat, "col", row_index // ratio).reshape(
        sequence_count, row_res, hidden
    )
    right_block = right_cols.reshape(sequence_count, col_res, hidden)
    group = math.gcd(row_res, max(1, 512 // col_res))
    blocks = row_res // group
    left_steps = jnp.transpose(
        left_rows.reshape(sequence_count, blocks, group, hidden), (1, 0, 2, 3)
    )
    grad_steps = pair_cotangent.reshape(blocks, group, col_res, pair_channels)
    per_homolog_weight = 1.0 / sequence_count

    def pair_step(carried, inputs):
        out_acc, right_acc = carried
        left_blk, grad_blk = inputs
        outer = (
            jnp.einsum("sic,sjd->ijcd", left_blk, right_block, preferred_element_type=jnp.float32)
            * per_homolog_weight
        )
        outer_bf = outer.reshape(group * col_res, hidden * hidden).astype(jnp.bfloat16)
        update = (
            jnp.dot(outer_bf, output_projection_matrix, preferred_element_type=jnp.float32)
            + output_bias
        ).astype(jnp.bfloat16)
        grad_rows = grad_blk.reshape(group * col_res, pair_channels)
        out_acc = out_acc + lax.dot_general(
            outer_bf, grad_rows, (((0,), (0,)), ((), ())), preferred_element_type=jnp.float32
        )
        outer_grad = jnp.dot(
            grad_rows, output_projection_matrix.T, preferred_element_type=jnp.float32
        ).astype(jnp.bfloat16)
        outer_grad = outer_grad.reshape(group, col_res, hidden, hidden)
        left_blk_grad = (
            jnp.einsum("ijcd,sjd->sic", outer_grad, right_block, preferred_element_type=jnp.float32)
            * per_homolog_weight
        )
        right_acc = (
            right_acc
            + jnp.einsum("ijcd,sic->sjd", outer_grad, left_blk, preferred_element_type=jnp.float32)
            * per_homolog_weight
        )
        return (
            (out_acc, right_acc),
            (update.reshape(group, col_res, pair_channels), left_blk_grad),
        )

    initial_carry = (
        jnp.zeros((hidden * hidden, pair_channels), jnp.float32),
        jnp.zeros((sequence_count, col_res, hidden), jnp.float32),
    )
    (out_acc, right_part), (updates, first_factor_pieces) = lax.scan(
        pair_step, initial_carry, (left_steps, grad_steps)
    )
    pair_delta = updates.reshape(row_res, col_res, pair_channels)
    left_part = jnp.transpose(first_factor_pieces, (1, 0, 2, 3)).reshape(
        sequence_count, row_res * hidden
    )
    right_flat = right_part.reshape(sequence_count, col_res * hidden)
    left_row = lax.psum(left_part, "col")
    owner = row_index // ratio == col_index
    slotted = lax.dynamic_update_slice_in_dim(
        jnp.zeros((sequence_count, col_res * hidden), jnp.float32),
        jnp.where(owner, left_row, 0.0),
        offset * hidden,
        1,
    )
    first_factor_total, right_sum = (
        lax.psum_scatter(slotted, "row", scatter_dimension=1, tiled=True),
        lax.psum_scatter(right_flat, "row", scatter_dimension=1, tiled=True),
    )
    left_bf = first_factor_total.reshape(sequence_count, local_residues, hidden).astype(
        jnp.bfloat16
    )
    right_bf = right_sum.reshape(sequence_count, local_residues, hidden).astype(jnp.bfloat16)
    normed_grad = jnp.dot(
        left_bf, first_factor_weights.T, preferred_element_type=jnp.float32
    ) + jnp.dot(right_bf, second_factor_weights.T, preferred_element_type=jnp.float32)
    scaled_gradient = normed_grad * standardize_multiplier
    centering_term = jnp.mean(scaled_gradient, axis=-1, keepdims=True)
    gradient_slope_term = jnp.mean(scaled_gradient * scaled_rows, axis=-1, keepdims=True)
    alignment_gradient = (
        reciprocal_deviation
        * (scaled_gradient - centering_term - scaled_rows * gradient_slope_term)
    ).astype(jnp.bfloat16)
    gain_part = jnp.sum(normed_grad * scaled_rows, axis=(0, 1))
    left_weight = jnp.einsum(
        "srm,srh->mh", normalized_rows, left_bf, preferred_element_type=jnp.float32
    )
    right_weight = jnp.einsum(
        "srm,srh->mh", normalized_rows, right_bf, preferred_element_type=jnp.float32
    )
    bias_part = jnp.sum(pair_cotangent, axis=(0, 1), dtype=jnp.float32)
    left_total, right_total, gain_total, bias_total = lax.psum(
        (left_weight, right_weight, gain_part, bias_part), ("row", "col")
    )
    out_share = lax.psum_scatter(out_acc, ("row", "col"), scatter_dimension=0, tiled=True)
    scale = 1.0 / (local_residues * row_count * col_count)
    return (
        pair_delta,
        alignment_gradient,
        gain_total * scale,
        left_total * scale,
        right_total * scale,
        out_share * scale,
        bias_total * scale,
    )


f32 = jnp.float32
bf16 = jnp.bfloat16


def mm(a, b):
    return lax.dot_general(a, b, (((1,), (0,)), ((), ())), preferred_element_type=f32)


def mm_t(a, b):
    return lax.dot_general(a, b, (((1,), (1,)), ((), ())), preferred_element_type=f32)


def factor_kernel(
    x_ref, gain_ref, w1_ref, w2_ref, cot_ref,
    wire_ref, send_ref, scaled_ref, normed_ref, recip_ref, diag_ref,
    rows, recips, twin, cots, moved,
):
    seqs, res, _ = x_ref.shape
    hidden = w1_ref.shape[0]
    columns = cot_ref.shape[1]
    devices = columns // res
    x = x_ref[...].astype(f32)
    centred = x - jnp.mean(x, axis=-1, keepdims=True)
    recip = lax.rsqrt(jnp.mean(centred * centred, axis=-1, keepdims=True) + ln_epsilon)
    rows[...] = centred * recip
    recips[...] = jnp.broadcast_to(recip, recips.shape)
    both = jnp.concatenate([w1_ref[...], w2_ref[...]], axis=0)
    low = lax.broadcasted_iota(jnp.int32, (hidden, 2 * seqs), 1) < seqs
    for r in range(res):
        scaled = rows[:, r, :]
        at = slice(r * seqs, (r + 1) * seqs)
        scaled_ref[at, :] = scaled
        recip_ref[at, :] = recips[:, r, :]
        normed = (scaled * gain_ref[...]).astype(bf16)
        normed_ref[at, :] = normed
        twin[...] = mm_t(both, jnp.concatenate([normed, normed], axis=0))
        even = twin[pl.ds(0, hidden, stride=2), :]
        odd = twin[pl.ds(1, hidden, stride=2), :]
        wire_ref[r * hidden : (r + 1) * hidden, :] = jnp.where(low, even, odd).astype(bf16)
        left = twin[:hidden, :]
        zero = jnp.zeros_like(left)
        lanes = slice(r * 2 * seqs, (r + 1) * 2 * seqs)
        diag_ref[:hidden, lanes] = jnp.where(low, left, zero).astype(bf16)
        diag_ref[hidden:, lanes] = jnp.where(low, zero, left).astype(bf16)
    for r in range(res):
        cots[r * columns : (r + 1) * columns, :] = cot_ref[r].astype(f32)
    for r in range(res):
        for q in range(res):
            block = cots[pl.ds(r * columns + q, devices, stride=res), :]
            moved[pl.ds(r * res + q, devices, stride=res * res), :] = block
    send_ref[...] = moved[...].astype(bf16)


def prepare_kernel(
    normed_ref, w1_ref, out_w_ref, cot_ref,
    mixed_ref, cot_t_ref, twin_w_ref, bias_ref,
    wide,
):
    hidden = w1_ref.shape[0]
    res = cot_ref.shape[0]
    pairs = out_w_ref.shape[1]
    seqs = normed_ref.shape[0] // res
    left = mm_t(normed_ref[...], w1_ref[...]).astype(bf16)
    wide[...] = out_w_ref[...].astype(f32)
    for d in range(hidden):
        w_d = wide[pl.ds(d, hidden, stride=hidden), :].astype(bf16)
        at = (d % 2) * hidden
        twin_w_ref[at : at + hidden, (d // 2) * pairs : (d // 2 + 1) * pairs] = w_d
        mixed = mm(left, w_d).astype(bf16)
        for r in range(res):
            mixed_ref[d * seqs : (d + 1) * seqs, r * pairs : (r + 1) * pairs] = mixed[
                r * seqs : (r + 1) * seqs, :
            ]
    total = jnp.zeros((1, pairs), f32)
    for r in range(res):
        cot = cot_ref[r].astype(f32)
        total = total + jnp.sum(cot, axis=0, keepdims=True)
        cot_t_ref[r * pairs : (r + 1) * pairs, :] = cot.T.astype(bf16)
    bias_ref[...] = jnp.broadcast_to(total, bias_ref.shape)


def pair_kernel(
    mine_ref, other_ref, mixed_ref, cot_t_ref, twin_w_ref, diag_ref, bias_ref,
    delta_ref, out_ref, sum_ref, lefts_ref,
    wide, rights, spread, outs,
):
    columns = rights.shape[0]
    lanes = mine_ref.shape[2]
    height = mine_ref.shape[1]
    half = mine_ref.shape[0]
    res = delta_ref.shape[0]
    pairs = delta_ref.shape[2]
    hidden = diag_ref.shape[0] // 2
    core = lax.rem(lax.axis_index("row"), 2)
    for b in range(half):
        device = (b % 4) * 8 + (b // 4) * 2
        at = pl.multiple_of((device + core) * height, height)
        wide[pl.ds(at, height), :] = mine_ref[b].astype(f32)
        at = pl.multiple_of((device + 1 - core) * height, height)
        wide[pl.ds(at, height), :] = other_ref[b].astype(f32)
    twins = hidden // 2
    for q in range(twins):
        here = slice(q * lanes, (q + 1) * lanes)
        lefts_ref[:, here] = wide[pl.ds(q, columns, stride=hidden), :].astype(bf16)
        rights[:, here] = wide[pl.ds(twins + q, columns, stride=hidden), :].astype(bf16)
    weight = 2.0 / lanes
    delta = mm(rights[...], mixed_ref[...]) * weight
    for r in range(res):
        delta_ref[r] = (delta[:, r * pairs : (r + 1) * pairs] + bias_ref[...]).astype(bf16)
        block = mm(cot_t_ref[r * pairs : (r + 1) * pairs, :], rights[...]).astype(bf16)
        for q in range(twins):
            spread[q * pairs : (q + 1) * pairs, r * lanes : (r + 1) * lanes] = block[
                :, q * lanes : (q + 1) * lanes
            ]
    grad = mm_t(diag_ref[...], spread[...]) * weight
    for d in range(hidden):
        at = (d % 2) * hidden
        outs[pl.ds(d, hidden, stride=hidden), :] = grad[
            at : at + hidden, (d // 2) * pairs : (d // 2 + 1) * pairs
        ]
    for c in range(hidden):
        place = int(format(c, "05b")[::-1], 2)
        out_ref[place * hidden : (place + 1) * hidden, :] = outs[
            c * hidden : (c + 1) * hidden, :
        ].astype(bf16)
    sum_ref[...] = mm(twin_w_ref[...], spread[...])


def input_kernel(
    lefts_ref, got_ref, out_w_ref, sum_ref, normed_ref, scaled_ref, recip_ref, gain_ref,
    w1_ref, w2_ref, bias_ref,
    grad_ref, small_ref,
    cots, spread, twin_w, rows,
):
    columns = lefts_ref.shape[0]
    seqs, res, channels = grad_ref.shape
    pairs = got_ref.shape[1]
    hidden = w1_ref.shape[0]
    lanes = 2 * seqs
    twins = hidden // 2
    cots[...] = got_ref[...].astype(f32)
    for q in range(twins):
        twin_w[:, q * pairs : (q + 1) * pairs] = out_w_ref[q * 2 * hidden : (q + 1) * 2 * hidden, :]
    for r in range(res):
        cot_t = cots[pl.ds(r, columns, stride=res), :].T.astype(bf16)
        block = mm(cot_t, lefts_ref[...]).astype(bf16)
        for q in range(twins):
            spread[q * pairs : (q + 1) * pairs, r * lanes : (r + 1) * lanes] = block[
                :, q * lanes : (q + 1) * lanes
            ]
    right_t = mm(twin_w[...], spread[...]).T
    left_t = sum_ref[...].T

    def untwin(t):
        parts = [
            t[r * lanes : r * lanes + seqs, :hidden] + t[r * lanes + seqs : (r + 1) * lanes, hidden:]
            for r in range(res)
        ]
        return jnp.concatenate(parts, axis=0) * (1.0 / seqs)

    left_sum = untwin(left_t)
    right_sum = untwin(right_t)
    left_bf = left_sum.astype(bf16)
    right_bf = right_sum.astype(bf16)
    normed_grad = mm(left_bf, w1_ref[...]) + mm(right_bf, w2_ref[...])
    scaled = scaled_ref[...]
    scaled_grad = normed_grad * gain_ref[...]
    centre = jnp.mean(scaled_grad, axis=-1, keepdims=True)
    slope = jnp.mean(scaled_grad * scaled, axis=-1, keepdims=True)
    grad = recip_ref[:, :1] * (scaled_grad - centre - scaled * slope)
    for r in range(res):
        rows[:, r, :] = grad[r * seqs : (r + 1) * seqs, :]
    grad_ref[...] = rows[...].astype(bf16)
    factors_t = jnp.concatenate([left_sum, right_sum], axis=1).T.astype(bf16)
    small_ref[: 2 * hidden, :] = mm(factors_t, normed_ref[...])
    gain_part = jnp.sum(normed_grad * scaled, axis=0, keepdims=True)
    bias_part = jnp.concatenate([bias_ref[:1, :]] * (channels // pairs), axis=1)
    line = lax.broadcasted_iota(jnp.int32, (8, channels), 0)
    small_ref[2 * hidden :, :] = jnp.where(
        line == 0, gain_part, jnp.where(line == 1, bias_part, jnp.zeros((8, channels), f32))
    )


def call(kernel, args, outs, scratch, flops, side):
    moved = sum(a.size * a.dtype.itemsize for a in args)
    return pl.pallas_call(
        kernel,
        out_shape=[jax.ShapeDtypeStruct(s, d) for s, d in outs],
        in_specs=[pl.BlockSpec(memory_space=pltpu.VMEM)] * len(args),
        out_specs=[pl.BlockSpec(memory_space=pltpu.VMEM)] * len(outs),
        scratch_shapes=[pltpu.VMEM(s, d) for s, d in scratch],
        compiler_params=pltpu.CompilerParams(vmem_limit_bytes=32 * 1024 * 1024),
        cost_estimate=pl.CostEstimate(flops=flops, bytes_accessed=moved, transcendentals=0),
        name=side,
    )(*args)


def swap(value, step):
    count = lax.axis_size("row")
    return lax.ppermute(value, "row", [(i, i ^ step) for i in range(count)])


def gather_digit(value, digit, base, unit):
    full = jnp.zeros((base,) + value.shape, value.dtype)
    full = lax.dynamic_update_index_in_dim(full, value, digit, 0)
    for k in range(1, base):
        full = lax.dynamic_update_index_in_dim(
            full, swap(value, k * unit), lax.bitwise_xor(digit, k), 0
        )
    return full


def on_device_row(
    homolog_features,
    standardize_multiplier,
    first_factor_weights,
    second_factor_weights,
    output_projection_matrix,
    output_bias,
    pair_cotangent,
):
    seqs, res, channels = homolog_features.shape
    hidden = first_factor_weights.shape[1]
    pairs = output_projection_matrix.shape[1]
    count = lax.axis_size("row")
    columns = res * count
    index = lax.axis_index("row")
    z, yx, core = index // 8, index // 2 % 4, index % 2
    own = seqs * res
    lanes = 2 * seqs
    gain = standardize_multiplier.reshape(1, channels)
    bias = output_bias.reshape(1, pairs)
    w1, w2 = first_factor_weights.T, second_factor_weights.T

    wire, send, scaled, normed, recip, diag = call(
        factor_kernel,
        (homolog_features, gain, w1, w2, pair_cotangent),
        [
            ((res * hidden, lanes), bf16),
            ((res * columns, pairs), bf16),
            ((own, channels), f32),
            ((own, channels), bf16),
            ((own, 128), f32),
            ((2 * hidden, res * lanes), bf16),
        ],
        [
            ((seqs, res, channels), f32),
            ((seqs, res, 128), f32),
            ((2 * hidden, lanes), f32),
            ((res * columns, pairs), f32),
            ((res * columns, pairs), f32),
        ],
        10**7,
        "factors",
    )
    got = lax.all_to_all(send, "row", 0, 0, tiled=True)
    plane = gather_digit(wire, z, 4, 8)
    mine = gather_digit(plane, yx, 4, 2).reshape(count // 2, res * hidden, lanes)
    other = swap(mine, 1)

    mixed, cot_t, twin_w, bias_part = call(
        prepare_kernel,
        (normed, w1, output_projection_matrix, pair_cotangent),
        [
            ((hidden * seqs, res * pairs), bf16),
            ((res * pairs, columns), bf16),
            ((2 * hidden, hidden // 2 * pairs), bf16),
            ((8, pairs), f32),
        ],
        [((hidden * hidden, pairs), f32)],
        10**8,
        "prepare",
    )
    delta, out_part, left_part, lefts = call(
        pair_kernel,
        (mine, other, mixed, cot_t, twin_w, diag, bias),
        [
            ((res, columns, pairs), bf16),
            ((hidden * hidden, pairs), bf16),
            ((2 * hidden, res * lanes), f32),
            ((columns, hidden * seqs), bf16),
        ],
        [
            ((columns * hidden, lanes), f32),
            ((columns, hidden * seqs), bf16),
            ((hidden // 2 * pairs, res * lanes), bf16),
            ((hidden * hidden, pairs), f32),
        ],
        10**9,
        "pairs",
    )
    grad, small = call(
        input_kernel,
        (
            lefts, got, output_projection_matrix, left_part, normed, scaled, recip, gain,
            w1, w2, bias_part,
        ),
        [((seqs, res, channels), bf16), ((2 * hidden + 8, channels), f32)],
        [
            ((columns * res, pairs), f32),
            ((hidden // 2 * pairs, res * lanes), bf16),
            ((2 * hidden, hidden // 2 * pairs), bf16),
            ((seqs, res, channels), f32),
        ],
        10**9,
        "inputs",
    )
    step = 1
    while step < count:
        bit = index // step % 2
        half = out_part.shape[0] // 2
        keep = lax.dynamic_slice_in_dim(out_part, bit * half, half, 0)
        give = lax.dynamic_slice_in_dim(out_part, (1 - bit) * half, half, 0)
        out_part = keep + swap(give, step)
        small = small + swap(small, step)
        step *= 2
    scale = 1.0 / columns
    small = small * scale
    return (
        delta,
        grad,
        small[2 * hidden],
        small[:hidden].T,
        small[hidden : 2 * hidden].T,
        out_part.astype(f32) * scale,
        small[2 * hidden + 1, :pairs],
    )


def solution(mesh):
    in_specs = (P(None, ("col", "row"), None), P(), P(), P(), P(), P(), P("row", "col", None))
    out_specs = (
        P("row", "col", None),
        P(None, ("col", "row"), None),
        P(),
        P(),
        P(),
        P(("row", "col"), None),
        P(),
    )
    one_row = mesh.shape["row"] == 32 and mesh.shape["col"] == 1
    body = on_device_row if one_row else on_device
    return jax.shard_map(
        body, mesh=mesh, in_specs=in_specs, out_specs=out_specs, check_vma=False
    )
```

```python
import functools
import math

import jax
import jax.numpy as jnp
from jax import lax
from jax.experimental import pallas as pl
from jax.experimental.pallas import tpu as pltpu
from jax.sharding import PartitionSpec as P

ln_epsilon = 1e-05


def from_root(value, axis, root):
    mine = lax.axis_index(axis) == root
    return lax.psum(jnp.where(mine, value, jnp.zeros_like(value)), axis)


def layer_norm_output(homolog_features, standardize_multiplier):
    value_entries = homolog_features.astype(jnp.float32)
    centred = value_entries - jnp.mean(value_entries, axis=-1, keepdims=True)
    reciprocal_deviation = lax.rsqrt(
        jnp.mean(centred * centred, axis=-1, keepdims=True) + ln_epsilon
    )
    scaled_rows = centred * reciprocal_deviation
    normalized_rows = (scaled_rows * standardize_multiplier).astype(jnp.bfloat16)
    return (scaled_rows, reciprocal_deviation, normalized_rows)


def on_device(
    homolog_features,
    standardize_multiplier,
    first_factor_weights,
    second_factor_weights,
    output_projection_matrix,
    output_bias,
    pair_cotangent,
):
    sequence_count, local_residues, channel_count = homolog_features.shape
    hidden = first_factor_weights.shape[1]
    pair_channels = output_projection_matrix.shape[1]
    row_count = lax.axis_size("row")
    col_count = lax.axis_size("col")
    ratio = row_count // col_count
    row_index = lax.axis_index("row")
    col_index = lax.axis_index("col")
    scaled_rows, reciprocal_deviation, normalized_rows = layer_norm_output(
        homolog_features, standardize_multiplier
    )
    left_own = jnp.dot(
        normalized_rows, first_factor_weights, preferred_element_type=jnp.float32
    ).astype(jnp.bfloat16)
    right_own = jnp.dot(
        normalized_rows, second_factor_weights, preferred_element_type=jnp.float32
    ).astype(jnp.bfloat16)
    left_cols, right_cols = (
        lax.all_gather(
            left_own.reshape(sequence_count, local_residues * hidden), "row", axis=1, tiled=True
        ),
        lax.all_gather(
            right_own.reshape(sequence_count, local_residues * hidden), "row", axis=1, tiled=True
        ),
    )
    col_res = local_residues * row_count
    row_res = col_res // ratio
    offset = row_index % ratio * row_res
    piece_flat = lax.dynamic_slice_in_dim(left_cols, offset * hidden, row_res * hidden, 1)
    left_rows = from_root(piece_flat, "col", row_index // ratio).reshape(
        sequence_count, row_res, hidden
    )
    right_block = right_cols.reshape(sequence_count, col_res, hidden)
    group = math.gcd(row_res, max(1, 512 // col_res))
    blocks = row_res // group
    left_steps = jnp.transpose(
        left_rows.reshape(sequence_count, blocks, group, hidden), (1, 0, 2, 3)
    )
    grad_steps = pair_cotangent.reshape(blocks, group, col_res, pair_channels)
    per_homolog_weight = 1.0 / sequence_count

    def pair_step(carried, inputs):
        out_acc, right_acc = carried
        left_blk, grad_blk = inputs
        outer = (
            jnp.einsum("sic,sjd->ijcd", left_blk, right_block, preferred_element_type=jnp.float32)
            * per_homolog_weight
        )
        outer_bf = outer.reshape(group * col_res, hidden * hidden).astype(jnp.bfloat16)
        update = (
            jnp.dot(outer_bf, output_projection_matrix, preferred_element_type=jnp.float32)
            + output_bias
        ).astype(jnp.bfloat16)
        grad_rows = grad_blk.reshape(group * col_res, pair_channels)
        out_acc = out_acc + lax.dot_general(
            outer_bf, grad_rows, (((0,), (0,)), ((), ())), preferred_element_type=jnp.float32
        )
        outer_grad = jnp.dot(
            grad_rows, output_projection_matrix.T, preferred_element_type=jnp.float32
        ).astype(jnp.bfloat16)
        outer_grad = outer_grad.reshape(group, col_res, hidden, hidden)
        left_blk_grad = (
            jnp.einsum("ijcd,sjd->sic", outer_grad, right_block, preferred_element_type=jnp.float32)
            * per_homolog_weight
        )
        right_acc = (
            right_acc
            + jnp.einsum("ijcd,sic->sjd", outer_grad, left_blk, preferred_element_type=jnp.float32)
            * per_homolog_weight
        )
        return (
            (out_acc, right_acc),
            (update.reshape(group, col_res, pair_channels), left_blk_grad),
        )

    initial_carry = (
        jnp.zeros((hidden * hidden, pair_channels), jnp.float32),
        jnp.zeros((sequence_count, col_res, hidden), jnp.float32),
    )
    (out_acc, right_part), (updates, first_factor_pieces) = lax.scan(
        pair_step, initial_carry, (left_steps, grad_steps)
    )
    pair_delta = updates.reshape(row_res, col_res, pair_channels)
    left_part = jnp.transpose(first_factor_pieces, (1, 0, 2, 3)).reshape(
        sequence_count, row_res * hidden
    )
    right_flat = right_part.reshape(sequence_count, col_res * hidden)
    left_row = lax.psum(left_part, "col")
    owner = row_index // ratio == col_index
    slotted = lax.dynamic_update_slice_in_dim(
        jnp.zeros((sequence_count, col_res * hidden), jnp.float32),
        jnp.where(owner, left_row, 0.0),
        offset * hidden,
        1,
    )
    first_factor_total, right_sum = (
        lax.psum_scatter(slotted, "row", scatter_dimension=1, tiled=True),
        lax.psum_scatter(right_flat, "row", scatter_dimension=1, tiled=True),
    )
    left_bf = first_factor_total.reshape(sequence_count, local_residues, hidden).astype(
        jnp.bfloat16
    )
    right_bf = right_sum.reshape(sequence_count, local_residues, hidden).astype(jnp.bfloat16)
    normed_grad = jnp.dot(
        left_bf, first_factor_weights.T, preferred_element_type=jnp.float32
    ) + jnp.dot(right_bf, second_factor_weights.T, preferred_element_type=jnp.float32)
    scaled_gradient = normed_grad * standardize_multiplier
    centering_term = jnp.mean(scaled_gradient, axis=-1, keepdims=True)
    gradient_slope_term = jnp.mean(scaled_gradient * scaled_rows, axis=-1, keepdims=True)
    alignment_gradient = (
        reciprocal_deviation
        * (scaled_gradient - centering_term - scaled_rows * gradient_slope_term)
    ).astype(jnp.bfloat16)
    gain_part = jnp.sum(normed_grad * scaled_rows, axis=(0, 1))
    left_weight = jnp.einsum(
        "srm,srh->mh", normalized_rows, left_bf, preferred_element_type=jnp.float32
    )
    right_weight = jnp.einsum(
        "srm,srh->mh", normalized_rows, right_bf, preferred_element_type=jnp.float32
    )
    bias_part = jnp.sum(pair_cotangent, axis=(0, 1), dtype=jnp.float32)
    left_total, right_total, gain_total, bias_total = lax.psum(
        (left_weight, right_weight, gain_part, bias_part), ("row", "col")
    )
    out_share = lax.psum_scatter(out_acc, ("row", "col"), scatter_dimension=0, tiled=True)
    scale = 1.0 / (local_residues * row_count * col_count)
    return (
        pair_delta,
        alignment_gradient,
        gain_total * scale,
        left_total * scale,
        right_total * scale,
        out_share * scale,
        bias_total * scale,
    )


f32 = jnp.float32
bf16 = jnp.bfloat16


def mm(a, b):
    return lax.dot_general(a, b, (((1,), (0,)), ((), ())), preferred_element_type=f32)


def mm_t(a, b):
    return lax.dot_general(a, b, (((1,), (1,)), ((), ())), preferred_element_type=f32)


def fetch(pairs, sems):
    copies = [pltpu.make_async_copy(a, b, sems.at[n]) for n, (a, b) in enumerate(pairs)]
    for copy in copies:
        copy.start()
    return copies


def factor_kernel(
    x_hbm, gain_hbm, w1_hbm, w2_hbm, cot_hbm,
    send0_ref, send1_ref, send2_ref, send3_ref, scaled_ref, normed_ref, recip_ref, diag_ref,
    x_ref, gain_ref, w1_ref, w2_ref, cot_ref, rows, recips, twin, cots, moved, sems,
):
    copies = fetch(
        [(x_hbm, x_ref), (gain_hbm, gain_ref), (w1_hbm, w1_ref), (w2_hbm, w2_ref), (cot_hbm, cot_ref)],
        sems,
    )
    sends = (send0_ref, send1_ref, send2_ref, send3_ref)
    seqs, res, _ = x_ref.shape
    hidden = w1_ref.shape[0]
    columns = cot_ref.shape[1]
    devices = columns // res
    copies[0].wait()
    x = x_ref[...].astype(f32)
    centred = x - jnp.mean(x, axis=-1, keepdims=True)
    recip = lax.rsqrt(jnp.mean(centred * centred, axis=-1, keepdims=True) + ln_epsilon)
    rows[...] = centred * recip
    recips[...] = jnp.broadcast_to(recip, recips.shape)
    for copy in copies[1:]:
        copy.wait()
    both = jnp.concatenate([w1_ref[...], w2_ref[...]], axis=0)
    low = lax.broadcasted_iota(jnp.int32, (hidden, 2 * seqs), 1) < seqs
    for r in range(res):
        scaled = rows[:, r, :]
        at = slice(r * seqs, (r + 1) * seqs)
        scaled_ref[at, :] = scaled
        recip_ref[at, :] = recips[:, r, :]
        normed = (scaled * gain_ref[...]).astype(bf16)
        normed_ref[at, :] = normed
        twin[r] = mm_t(both, jnp.concatenate([normed, normed], axis=0))
        even = twin[r, pl.ds(0, hidden, stride=2), :]
        odd = twin[r, pl.ds(1, hidden, stride=2), :]
        piece = jnp.where(low, even, odd).astype(bf16)
        for send_ref in sends:
            send_ref[r * hidden : (r + 1) * hidden, :] = piece
        left = twin[r, :hidden, :]
        zero = jnp.zeros_like(left)
        lanes = slice(r * 2 * seqs, (r + 1) * 2 * seqs)
        diag_ref[:hidden, lanes] = jnp.where(low, left, zero).astype(bf16)
        diag_ref[hidden:, lanes] = jnp.where(low, zero, left).astype(bf16)
    for r in range(res):
        cots[r * columns : (r + 1) * columns, :] = cot_ref[r].astype(f32)
    for r in range(res):
        for q in range(res):
            block = cots[pl.ds(r * columns + q, devices, stride=res), :]
            moved[pl.ds(r * res + q, devices, stride=res * res), :] = block
    index = lax.axis_index("row")
    per = res * res
    plane = devices // len(sends)
    for n in range(devices):
        at = pl.multiple_of(lax.bitwise_xor(index, n) * per, per)
        to = res * hidden + n % plane * per
        sends[n // plane][to : to + per, :] = moved[pl.ds(at, per), :].astype(bf16)


def pack_kernel(height, *refs):
    held, sent = refs[: len(refs) // 2], refs[len(refs) // 2 :]
    cut = (held[0].shape[0] - height) // len(sent)
    for z, h in enumerate(held):
        factors = h[:height, :]
        for yx, s in enumerate(sent):
            s[z * height : (z + 1) * height, :] = factors
            to = len(held) * height + z * cut
            s[to : to + cut, :] = h[height + yx * cut : height + (yx + 1) * cut, :]


def prepare_kernel(
    out_w_ref, cot_ref,
    cot_t_ref, twin_left_ref, twin_right_ref, bias_ref,
    wide,
):
    hidden = twin_left_ref.shape[0] // 2
    res, columns, pairs = cot_ref.shape
    wide[...] = out_w_ref[...].astype(f32)
    for d in range(hidden):
        at = (d % 2) * hidden
        twin_left_ref[at : at + hidden, (d // 2) * pairs : (d // 2 + 1) * pairs] = wide[
            pl.ds(d, hidden, stride=hidden), :
        ].astype(bf16)
    for q in range(hidden // 2):
        twin_right_ref[:, q * pairs : (q + 1) * pairs] = out_w_ref[
            q * 2 * hidden : (q + 1) * 2 * hidden, :
        ]
    total = jnp.zeros((1, pairs), f32)
    for r in range(res):
        cot = cot_ref[r].astype(f32)
        total = total + jnp.sum(cot, axis=0, keepdims=True)
        cot_t_ref[r * pairs : (r + 1) * pairs, :] = cot.T.astype(bf16)
    bias_ref[...] = jnp.broadcast_to(total, bias_ref.shape)


def sums_kernel(
    mine_ref, other_ref, cot_t_ref, twin_left_ref, twin_right_ref, normed_ref, scaled_ref,
    w1_ref, w2_ref, bias_ref,
    small_ref, rights_ref, spread_ref, grad_ref,
    wide, lefts, turned, cots, got_t,
):
    columns = rights_ref.shape[0]
    yxs, _, lanes = mine_ref.shape
    seqs = lanes // 2
    channels = normed_ref.shape[1]
    hidden = w1_ref.shape[0]
    twins = hidden // 2
    pairs = bias_ref.shape[1]
    res = spread_ref.shape[1] // lanes
    index = lax.axis_index("row")
    height = res * hidden
    per = res * res
    zs = wide.shape[0] // (2 * yxs * height)
    for yx in range(yxs):
        for z in range(zs):
            factors = slice(z * height, (z + 1) * height)
            first = zs * height + z * 2 * per
            for core, ref in enumerate((mine_ref, other_ref)):
                device = lax.bitwise_xor(index, z * 2 * yxs + yx * 2 + core)
                at = pl.multiple_of(device * height, height)
                wide[pl.ds(at, height), :] = ref[yx, factors, :].astype(f32)
                block = ref[yx, first + core * per : first + (core + 1) * per, :]
                at = pl.multiple_of(device * per, per)
                cots[pl.ds(at, per), :] = block.astype(f32)
    for r in range(res):
        got_t[r * pairs : (r + 1) * pairs, :] = cots[pl.ds(r, columns, stride=res), :].T.astype(bf16)
    for q in range(twins):
        here = slice(q * lanes, (q + 1) * lanes)
        lefts[:, here] = wide[pl.ds(q, columns, stride=hidden), :].astype(bf16)
        rights_ref[:, here] = wide[pl.ds(twins + q, columns, stride=hidden), :].astype(bf16)

    def summed(cots, factors, weights, out):
        for r in range(res):
            block = mm(cots[r * pairs : (r + 1) * pairs, :], factors[...]).astype(bf16)
            for q in range(twins):
                out[q * pairs : (q + 1) * pairs, r * lanes : (r + 1) * lanes] = block[
                    :, q * lanes : (q + 1) * lanes
                ]
        t = mm(weights[...], out[...]).T
        parts = [
            t[r * lanes : r * lanes + seqs, :hidden] + t[r * lanes + seqs : (r + 1) * lanes, hidden:]
            for r in range(res)
        ]
        return jnp.concatenate(parts, axis=0) * (1.0 / seqs)

    left_sum = summed(cot_t_ref, rights_ref, twin_left_ref, spread_ref)
    right_sum = summed(got_t, lefts, twin_right_ref, turned)
    normed_grad = mm(left_sum.astype(bf16), w1_ref[...]) + mm(right_sum.astype(bf16), w2_ref[...])
    grad_ref[...] = normed_grad
    factors_t = jnp.concatenate([left_sum, right_sum], axis=1).T.astype(bf16)
    small_ref[: 2 * hidden, :] = mm(factors_t, normed_ref[...])
    gain_part = jnp.sum(normed_grad * scaled_ref[...], axis=0, keepdims=True)
    bias_part = jnp.concatenate([bias_ref[:1, :]] * (channels // pairs), axis=1)
    line = lax.broadcasted_iota(jnp.int32, (16, channels), 0)
    small_ref[2 * hidden :, :] = jnp.where(
        line == 0, gain_part, jnp.where(line == 1, bias_part, jnp.zeros((16, channels), f32))
    )


def share_kernel(res, diag_ref, spread_ref, out_ref, outs):
    hidden = diag_ref.shape[0] // 2
    pairs = out_ref.shape[1]
    seqs = diag_ref.shape[1] // (2 * res)
    grad = mm_t(diag_ref[...], spread_ref[...]) * (1.0 / seqs)
    for d in range(hidden):
        at = (d % 2) * hidden
        outs[pl.ds(d, hidden, stride=hidden), :] = grad[
            at : at + hidden, (d // 2) * pairs : (d // 2 + 1) * pairs
        ]
    index = lax.axis_index("row")
    for place in range(hidden):
        chunk = lax.bitwise_xor(index, int(format(place, "05b")[::-1], 2))
        at = pl.multiple_of(chunk * hidden, hidden)
        out_ref[place * hidden : (place + 1) * hidden, :] = outs[pl.ds(at, hidden), :]


def result_kernel(
    rights_ref, twin_left_ref, w1_ref, normed_ref, bias_ref, normed_grad_ref, scaled_ref, recip_ref, gain_ref,
    delta_ref, grad_ref,
    rows, mixed,
):
    res, _, pairs = delta_ref.shape
    seqs = grad_ref.shape[0]
    hidden = w1_ref.shape[0]
    left = mm_t(normed_ref[...], w1_ref[...]).astype(bf16)
    for d in range(hidden):
        at = (d % 2) * hidden
        part = mm(left, twin_left_ref[at : at + hidden, (d // 2) * pairs : (d // 2 + 1) * pairs])
        part = part.astype(bf16)
        for r in range(res):
            mixed[d * seqs : (d + 1) * seqs, r * pairs : (r + 1) * pairs] = part[
                r * seqs : (r + 1) * seqs, :
            ]
    delta = mm(rights_ref[...], mixed[...]) * (1.0 / seqs)
    for r in range(res):
        delta_ref[r] = (delta[:, r * pairs : (r + 1) * pairs] + bias_ref[...]).astype(bf16)
    scaled = scaled_ref[...]
    scaled_grad = normed_grad_ref[...] * gain_ref[...]
    centre = jnp.mean(scaled_grad, axis=-1, keepdims=True)
    slope = jnp.mean(scaled_grad * scaled, axis=-1, keepdims=True)
    grad = recip_ref[:, :1] * (scaled_grad - centre - scaled * slope)
    for r in range(res):
        rows[:, r, :] = grad[r * seqs : (r + 1) * seqs, :]
    grad_ref[...] = rows[...].astype(bf16)


def finish_kernel(
    scale, own_ref, came_ref, keep_ref, shared_ref,
    gain_hbm, left_hbm, right_hbm, out_hbm, bias_hbm,
    total, out, sems,
):
    hidden = left_hbm.shape[0]
    pairs = bias_hbm.shape[1]
    total[...] = (own_ref[...].astype(f32) + came_ref[...].astype(f32)) * scale
    out[...] = (keep_ref[...] + shared_ref[...].astype(f32)) * scale
    copies = fetch(
        [
            (total.at[2 * hidden : 2 * hidden + 1, :], gain_hbm),
            (total.at[:hidden, :], left_hbm),
            (total.at[hidden : 2 * hidden, :], right_hbm),
            (out, out_hbm),
            (total.at[2 * hidden + 1 : 2 * hidden + 2, :pairs], bias_hbm),
        ],
        sems,
    )
    for copy in copies:
        copy.wait()


def call(kernel, name, args, outs, scratch, flops, remote_in=False, remote_out=False, vmem=16):
    moved = sum(a.size * a.dtype.itemsize for a in args)
    space = lambda far: pl.BlockSpec(memory_space=pltpu.HBM if far else pltpu.VMEM)
    sems = max(len(args) * remote_in, len(outs) * remote_out)
    shapes = [pltpu.VMEM(s, d) for s, d in scratch]
    if sems:
        shapes.append(pltpu.SemaphoreType.DMA((sems,)))
    return pl.pallas_call(
        kernel,
        out_shape=[jax.ShapeDtypeStruct(s, d) for s, d in outs],
        in_specs=[space(remote_in)] * len(args),
        out_specs=[space(remote_out)] * len(outs),
        scratch_shapes=shapes,
        compiler_params=pltpu.CompilerParams(vmem_limit_bytes=vmem * 1024 * 1024),
        cost_estimate=pl.CostEstimate(flops=flops, bytes_accessed=moved, transcendentals=0),
        name=name,
    )(*args)


def swap(value, step):
    count = lax.axis_size("row")
    return lax.ppermute(value, "row", [(i, i ^ step) for i in range(count)])


def on_device_row(
    homolog_features,
    standardize_multiplier,
    first_factor_weights,
    second_factor_weights,
    output_projection_matrix,
    output_bias,
    pair_cotangent,
):
    seqs, res, channels = homolog_features.shape
    hidden = first_factor_weights.shape[1]
    pairs = output_projection_matrix.shape[1]
    count = lax.axis_size("row")
    columns = res * count
    own = seqs * res
    lanes = 2 * seqs
    twins = hidden // 2
    gain = standardize_multiplier.reshape(1, channels)
    bias = output_bias.reshape(1, pairs)
    w1, w2 = first_factor_weights.T, second_factor_weights.T
    wide = (2 * hidden, twins * pairs)

    zs, yxs = 4, 4
    height = res * hidden
    *sends, scaled, normed, recip, diag = call(
        factor_kernel,
        "factors",
        (homolog_features, gain, w1, w2, pair_cotangent),
        [
            *[((height + res * columns // zs, lanes), bf16)] * zs,
            ((own, channels), f32),
            ((own, channels), bf16),
            ((own, 128), f32),
            ((2 * hidden, res * lanes), bf16),
        ],
        [
            ((seqs, res, channels), bf16),
            ((1, channels), f32),
            ((hidden, channels), bf16),
            ((hidden, channels), bf16),
            ((res, columns, pairs), bf16),
            ((seqs, res, channels), f32),
            ((seqs, res, 128), f32),
            ((res, 2 * hidden, lanes), f32),
            ((res * columns, pairs), f32),
            ((res * columns, pairs), f32),
        ],
        10**6,
        remote_in=True,
        vmem=60,
    )
    swapped = {z: swap(sends[z], z * 2 * yxs) for z in (3, 2, 1)}
    sent = call(
        functools.partial(pack_kernel, height),
        "pack",
        [sends[0]] + [swapped[z] for z in range(1, zs)],
        [((zs * height + zs * 2 * res * res, lanes), bf16)] * yxs,
        [],
        10**6,
    )
    mine = jnp.stack([sent[0]] + [swap(sent[yx], yx * 2) for yx in range(1, yxs)])
    other = swap(mine, 1)
    cot_t, twin_left, twin_right, bias_part = call(
        prepare_kernel,
        "prepare",
        (output_projection_matrix, pair_cotangent),
        [
            ((res * pairs, columns), bf16),
            (wide, bf16),
            (wide, bf16),
            ((8, pairs), f32),
        ],
        [((hidden * hidden, pairs), f32)],
        10**6,
    )
    small, rights, spread, normed_grad = call(
        sums_kernel,
        "sums",
        (
            mine, other, cot_t, twin_left, twin_right, normed, scaled, w1, w2, bias_part,
        ),
        [
            ((2 * hidden + 16, channels), f32),
            ((columns, hidden * seqs), bf16),
            ((twins * pairs, res * lanes), bf16),
            ((own, channels), f32),
        ],
        [
            ((columns * hidden, lanes), f32),
            ((columns, hidden * seqs), bf16),
            ((twins * pairs, res * lanes), bf16),
            ((res * columns, pairs), f32),
            ((res * pairs, columns), bf16),
        ],
        10**6,
    )
    (out_part,) = call(
        functools.partial(share_kernel, res),
        "shares",
        (diag, spread),
        [((hidden * hidden, pairs), f32)],
        [((hidden * hidden, pairs), f32)],
        10**6,
    )
    delta, grad = call(
        result_kernel,
        "results",
        (rights, twin_left, w1, normed, bias, normed_grad, scaled, recip, gain),
        [((res, columns, pairs), bf16), ((seqs, res, channels), bf16)],
        [((seqs, res, channels), f32), ((hidden * seqs, res * pairs), bf16)],
        10**6,
    )
    half = hidden * hidden // 2
    small = (small + swap(small, 1)).astype(bf16)
    step = 1
    while step < count:
        keep, give = out_part[:half], out_part[half:].astype(bf16)
        if 2 * step < count:
            out_part = keep + swap(give, step).astype(f32)
        if step > 1:
            small = lax.optimization_barrier(small)
            came = swap(small, step + 1)
            if 2 * step < count:
                small = small + came
            if step == 2:
                small, delta, grad = lax.optimization_barrier((small, delta, grad))
        step *= 2
        half //= 2
    shared = swap(give, count // 2)
    gain_out, left_out, right_out, out_share, bias_out = call(
        functools.partial(finish_kernel, 1.0 / columns),
        "finish",
        (small, came, keep, shared),
        [
            ((1, channels), f32),
            ((hidden, channels), f32),
            ((hidden, channels), f32),
            ((hidden * hidden // count, pairs), f32),
            ((1, pairs), f32),
        ],
        [((2 * hidden + 16, channels), f32), ((hidden * hidden // count, pairs), f32)],
        10**6,
        remote_out=True,
    )
    return (
        delta,
        grad,
        gain_out.reshape(channels),
        left_out.T,
        right_out.T,
        out_share,
        bias_out.reshape(pairs),
    )


def solution(mesh):
    in_specs = (P(None, ("col", "row"), None), P(), P(), P(), P(), P(), P("row", "col", None))
    out_specs = (
        P("row", "col", None),
        P(None, ("col", "row"), None),
        P(),
        P(),
        P(),
        P(("row", "col"), None),
        P(),
    )
    one_row = mesh.shape["row"] == 32 and mesh.shape["col"] == 1
    body = on_device_row if one_row else on_device
    return jax.shard_map(
        body, mesh=mesh, in_specs=in_specs, out_specs=out_specs, check_vma=False
    )
```

```python
import functools
import math

import jax
import jax.numpy as jnp
from jax import lax
from jax.experimental import pallas as pl
from jax.experimental.pallas import tpu as pltpu
from jax.sharding import PartitionSpec as P

ln_epsilon = 1e-05


def from_root(value, axis, root):
    mine = lax.axis_index(axis) == root
    return lax.psum(jnp.where(mine, value, jnp.zeros_like(value)), axis)


def layer_norm_output(homolog_features, standardize_multiplier):
    value_entries = homolog_features.astype(jnp.float32)
    centred = value_entries - jnp.mean(value_entries, axis=-1, keepdims=True)
    reciprocal_deviation = lax.rsqrt(
        jnp.mean(centred * centred, axis=-1, keepdims=True) + ln_epsilon
    )
    scaled_rows = centred * reciprocal_deviation
    normalized_rows = (scaled_rows * standardize_multiplier).astype(jnp.bfloat16)
    return (scaled_rows, reciprocal_deviation, normalized_rows)


def on_device(
    homolog_features,
    standardize_multiplier,
    first_factor_weights,
    second_factor_weights,
    output_projection_matrix,
    output_bias,
    pair_cotangent,
):
    sequence_count, local_residues, channel_count = homolog_features.shape
    hidden = first_factor_weights.shape[1]
    pair_channels = output_projection_matrix.shape[1]
    row_count = lax.axis_size("row")
    col_count = lax.axis_size("col")
    ratio = row_count // col_count
    row_index = lax.axis_index("row")
    col_index = lax.axis_index("col")
    scaled_rows, reciprocal_deviation, normalized_rows = layer_norm_output(
        homolog_features, standardize_multiplier
    )
    left_own = jnp.dot(
        normalized_rows, first_factor_weights, preferred_element_type=jnp.float32
    ).astype(jnp.bfloat16)
    right_own = jnp.dot(
        normalized_rows, second_factor_weights, preferred_element_type=jnp.float32
    ).astype(jnp.bfloat16)
    left_cols, right_cols = (
        lax.all_gather(
            left_own.reshape(sequence_count, local_residues * hidden), "row", axis=1, tiled=True
        ),
        lax.all_gather(
            right_own.reshape(sequence_count, local_residues * hidden), "row", axis=1, tiled=True
        ),
    )
    col_res = local_residues * row_count
    row_res = col_res // ratio
    offset = row_index % ratio * row_res
    piece_flat = lax.dynamic_slice_in_dim(left_cols, offset * hidden, row_res * hidden, 1)
    left_rows = from_root(piece_flat, "col", row_index // ratio).reshape(
        sequence_count, row_res, hidden
    )
    right_block = right_cols.reshape(sequence_count, col_res, hidden)
    group = math.gcd(row_res, max(1, 512 // col_res))
    blocks = row_res // group
    left_steps = jnp.transpose(
        left_rows.reshape(sequence_count, blocks, group, hidden), (1, 0, 2, 3)
    )
    grad_steps = pair_cotangent.reshape(blocks, group, col_res, pair_channels)
    per_homolog_weight = 1.0 / sequence_count

    def pair_step(carried, inputs):
        out_acc, right_acc = carried
        left_blk, grad_blk = inputs
        outer = (
            jnp.einsum("sic,sjd->ijcd", left_blk, right_block, preferred_element_type=jnp.float32)
            * per_homolog_weight
        )
        outer_bf = outer.reshape(group * col_res, hidden * hidden).astype(jnp.bfloat16)
        update = (
            jnp.dot(outer_bf, output_projection_matrix, preferred_element_type=jnp.float32)
            + output_bias
        ).astype(jnp.bfloat16)
        grad_rows = grad_blk.reshape(group * col_res, pair_channels)
        out_acc = out_acc + lax.dot_general(
            outer_bf, grad_rows, (((0,), (0,)), ((), ())), preferred_element_type=jnp.float32
        )
        outer_grad = jnp.dot(
            grad_rows, output_projection_matrix.T, preferred_element_type=jnp.float32
        ).astype(jnp.bfloat16)
        outer_grad = outer_grad.reshape(group, col_res, hidden, hidden)
        left_blk_grad = (
            jnp.einsum("ijcd,sjd->sic", outer_grad, right_block, preferred_element_type=jnp.float32)
            * per_homolog_weight
        )
        right_acc = (
            right_acc
            + jnp.einsum("ijcd,sic->sjd", outer_grad, left_blk, preferred_element_type=jnp.float32)
            * per_homolog_weight
        )
        return (
            (out_acc, right_acc),
            (update.reshape(group, col_res, pair_channels), left_blk_grad),
        )

    initial_carry = (
        jnp.zeros((hidden * hidden, pair_channels), jnp.float32),
        jnp.zeros((sequence_count, col_res, hidden), jnp.float32),
    )
    (out_acc, right_part), (updates, first_factor_pieces) = lax.scan(
        pair_step, initial_carry, (left_steps, grad_steps)
    )
    pair_delta = updates.reshape(row_res, col_res, pair_channels)
    left_part = jnp.transpose(first_factor_pieces, (1, 0, 2, 3)).reshape(
        sequence_count, row_res * hidden
    )
    right_flat = right_part.reshape(sequence_count, col_res * hidden)
    left_row = lax.psum(left_part, "col")
    owner = row_index // ratio == col_index
    slotted = lax.dynamic_update_slice_in_dim(
        jnp.zeros((sequence_count, col_res * hidden), jnp.float32),
        jnp.where(owner, left_row, 0.0),
        offset * hidden,
        1,
    )
    first_factor_total, right_sum = (
        lax.psum_scatter(slotted, "row", scatter_dimension=1, tiled=True),
        lax.psum_scatter(right_flat, "row", scatter_dimension=1, tiled=True),
    )
    left_bf = first_factor_total.reshape(sequence_count, local_residues, hidden).astype(
        jnp.bfloat16
    )
    right_bf = right_sum.reshape(sequence_count, local_residues, hidden).astype(jnp.bfloat16)
    normed_grad = jnp.dot(
        left_bf, first_factor_weights.T, preferred_element_type=jnp.float32
    ) + jnp.dot(right_bf, second_factor_weights.T, preferred_element_type=jnp.float32)
    scaled_gradient = normed_grad * standardize_multiplier
    centering_term = jnp.mean(scaled_gradient, axis=-1, keepdims=True)
    gradient_slope_term = jnp.mean(scaled_gradient * scaled_rows, axis=-1, keepdims=True)
    alignment_gradient = (
        reciprocal_deviation
        * (scaled_gradient - centering_term - scaled_rows * gradient_slope_term)
    ).astype(jnp.bfloat16)
    gain_part = jnp.sum(normed_grad * scaled_rows, axis=(0, 1))
    left_weight = jnp.einsum(
        "srm,srh->mh", normalized_rows, left_bf, preferred_element_type=jnp.float32
    )
    right_weight = jnp.einsum(
        "srm,srh->mh", normalized_rows, right_bf, preferred_element_type=jnp.float32
    )
    bias_part = jnp.sum(pair_cotangent, axis=(0, 1), dtype=jnp.float32)
    left_total, right_total, gain_total, bias_total = lax.psum(
        (left_weight, right_weight, gain_part, bias_part), ("row", "col")
    )
    out_share = lax.psum_scatter(out_acc, ("row", "col"), scatter_dimension=0, tiled=True)
    scale = 1.0 / (local_residues * row_count * col_count)
    return (
        pair_delta,
        alignment_gradient,
        gain_total * scale,
        left_total * scale,
        right_total * scale,
        out_share * scale,
        bias_total * scale,
    )


f32 = jnp.float32
bf16 = jnp.bfloat16


def mm(a, b):
    return lax.dot_general(a, b, (((1,), (0,)), ((), ())), preferred_element_type=f32)


def mm_t(a, b):
    return lax.dot_general(a, b, (((1,), (1,)), ((), ())), preferred_element_type=f32)


def fetch(pairs, sems):
    copies = [pltpu.make_async_copy(a, b, sems.at[n]) for n, (a, b) in enumerate(pairs)]
    for copy in copies:
        copy.start()
    return copies


def factor_kernel(
    x_hbm, gain_hbm, w1_hbm, w2_hbm, cot_hbm,
    send0_ref, send1_ref, send2_ref, send3_ref, scaled_ref, normed_ref, recip_ref, diag_ref,
    x_ref, gain_ref, w1_ref, w2_ref, cot_ref, rows, twin, cots, moved, sems,
):
    copies = fetch(
        [(x_hbm, x_ref), (gain_hbm, gain_ref), (w1_hbm, w1_ref), (w2_hbm, w2_ref), (cot_hbm, cot_ref)],
        sems,
    )
    sends = (send0_ref, send1_ref, send2_ref, send3_ref)
    seqs, res, _ = x_ref.shape
    hidden = w1_ref.shape[0]
    columns = cot_ref.shape[1]
    devices = columns // res
    copies[0].wait()
    rows[...] = x_ref[...].astype(f32)
    for copy in copies[1:]:
        copy.wait()
    both = jnp.concatenate([w1_ref[...], w2_ref[...]], axis=0)
    low = lax.broadcasted_iota(jnp.int32, (hidden, 2 * seqs), 1) < seqs
    for r in range(res):
        x = rows[:, r, :]
        centred = x - jnp.mean(x, axis=-1, keepdims=True)
        recip = lax.rsqrt(jnp.mean(centred * centred, axis=-1, keepdims=True) + ln_epsilon)
        scaled = centred * recip
        at = slice(r * seqs, (r + 1) * seqs)
        scaled_ref[at, :] = scaled
        recip_ref[at, :] = jnp.broadcast_to(recip, (seqs, recip_ref.shape[1]))
        normed = (scaled * gain_ref[...]).astype(bf16)
        normed_ref[at, :] = normed
        twin[r] = mm_t(both, jnp.concatenate([normed, normed], axis=0))
        even = twin[r, pl.ds(0, hidden, stride=2), :]
        odd = twin[r, pl.ds(1, hidden, stride=2), :]
        piece = jnp.where(low, even, odd).astype(bf16)
        for send_ref in sends:
            send_ref[r * hidden : (r + 1) * hidden, :] = piece
        left = twin[r, :hidden, :]
        zero = jnp.zeros_like(left)
        lanes = slice(r * 2 * seqs, (r + 1) * 2 * seqs)
        diag_ref[:hidden, lanes] = jnp.where(low, left, zero).astype(bf16)
        diag_ref[hidden:, lanes] = jnp.where(low, zero, left).astype(bf16)
    for r in range(res):
        cots[r * columns : (r + 1) * columns, :] = cot_ref[r].astype(f32)
    for r in range(res):
        for q in range(res):
            block = cots[pl.ds(r * columns + q, devices, stride=res), :]
            at = (r * res + q) * (devices + 1)
            moved[at : at + devices, :] = block
    index = lax.axis_index("row")
    per = res * res
    plane = devices // len(sends)
    for n in range(devices):
        block = moved[pl.ds(lax.bitwise_xor(index, n), per, stride=devices + 1), :]
        to = res * hidden + n % plane * per
        sends[n // plane][to : to + per, :] = block.astype(bf16)


def own_kernel(*refs):
    for a, b in zip(refs[: len(refs) // 2], refs[len(refs) // 2 :]):
        b[...] = a[...]


def pack_kernel(height, *refs):
    held, sent = refs[: len(refs) // 2], refs[len(refs) // 2 :]
    cut = (held[0].shape[0] - height) // len(sent)
    for z, h in enumerate(held):
        factors = h[:height, :]
        for yx, s in enumerate(sent):
            s[z * height : (z + 1) * height, :] = factors
            to = len(held) * height + z * cut
            s[to : to + cut, :] = h[height + yx * cut : height + (yx + 1) * cut, :]


def prepare_kernel(
    out_w_ref, cot_ref, scaled_in, w1_in, w2_in,
    cot_t_ref, twin_left_ref, twin_right_ref, bias_ref, scaled_ref, w1_ref, w2_ref,
    wide,
):
    hidden = twin_left_ref.shape[0] // 2
    res, columns, pairs = cot_ref.shape
    own_kernel(scaled_in, w1_in, w2_in, scaled_ref, w1_ref, w2_ref)
    wide[...] = out_w_ref[...].astype(f32)
    for d in range(hidden):
        at = (d % 2) * hidden
        twin_left_ref[at : at + hidden, (d // 2) * pairs : (d // 2 + 1) * pairs] = wide[
            pl.ds(d, hidden, stride=hidden), :
        ].astype(bf16)
    for q in range(hidden // 2):
        twin_right_ref[:, q * pairs : (q + 1) * pairs] = out_w_ref[
            q * 2 * hidden : (q + 1) * 2 * hidden, :
        ]
    total = jnp.zeros((1, pairs), f32)
    for r in range(res):
        cot = cot_ref[r].astype(f32)
        total = total + jnp.sum(cot, axis=0, keepdims=True)
        cot_t_ref[r * pairs : (r + 1) * pairs, :] = cot.T.astype(bf16)
    bias_ref[...] = jnp.broadcast_to(total, bias_ref.shape)


def sums_kernel(
    yxs, cot_t_ref, twin_left_ref, twin_right_ref, normed_ref, scaled_ref,
    w1_ref, w2_ref, bias_ref, *refs,
):
    mine, other = refs[:yxs], refs[yxs : 2 * yxs]
    small_ref, rights_ref, spread_ref, grad_ref, wide, lefts, turned, cots, got_t = refs[2 * yxs :]
    columns = rights_ref.shape[0]
    lanes = mine[0].shape[1]
    seqs = lanes // 2
    channels = normed_ref.shape[1]
    hidden = w1_ref.shape[0]
    twins = hidden // 2
    pairs = bias_ref.shape[1]
    res = spread_ref.shape[1] // lanes
    index = lax.axis_index("row")
    height = res * hidden
    per = res * res
    zs = columns // (2 * yxs * res)
    for yx in range(yxs):
        for z in range(zs):
            factors = slice(z * height, (z + 1) * height)
            first = zs * height + z * 2 * per
            for core, ref in enumerate((mine[yx], other[yx])):
                device = lax.bitwise_xor(index, z * 2 * yxs + yx * 2 + core)
                block = ref[factors, :].astype(f32)
                for r in range(res):
                    wide[pl.ds(device * res + r, hidden, stride=columns + 1), :] = block[
                        r * hidden : (r + 1) * hidden
                    ]
                block = ref[first + core * per : first + (core + 1) * per, :]
                at = pl.multiple_of(device * per, per)
                cots[pl.ds(at, per), :] = block.astype(f32)
    for r in range(res):
        got_t[r * pairs : (r + 1) * pairs, :] = cots[pl.ds(r, columns, stride=res), :].T.astype(bf16)
    for q in range(twins):
        here = slice(q * lanes, (q + 1) * lanes)
        at = q * (columns + 1)
        lefts[:, here] = wide[at : at + columns, :].astype(bf16)
        at = (twins + q) * (columns + 1)
        rights_ref[:, here] = wide[at : at + columns, :].astype(bf16)

    def summed(cots, factors, weights, out):
        for q in range(0, twins, 2):
            block = mm(cots[...], factors[:, q * lanes : (q + 2) * lanes]).astype(bf16)
            for r in range(res):
                for e in range(2):
                    out[(q + e) * pairs : (q + e + 1) * pairs, r * lanes : (r + 1) * lanes] = block[
                        r * pairs : (r + 1) * pairs, e * lanes : (e + 1) * lanes
                    ]
        t = mm(weights[...], out[...]).T
        parts = [
            t[r * lanes : r * lanes + seqs, :hidden] + t[r * lanes + seqs : (r + 1) * lanes, hidden:]
            for r in range(res)
        ]
        return jnp.concatenate(parts, axis=0) * (1.0 / seqs)

    left_sum = summed(cot_t_ref, rights_ref, twin_left_ref, spread_ref)
    right_sum = summed(got_t, lefts, twin_right_ref, turned)
    normed_grad = mm(left_sum.astype(bf16), w1_ref[...]) + mm(right_sum.astype(bf16), w2_ref[...])
    grad_ref[...] = normed_grad
    factors_t = jnp.concatenate([left_sum, right_sum], axis=1).T.astype(bf16)
    weights = mm(factors_t, normed_ref[...])
    gain_part = jnp.sum(normed_grad * scaled_ref[...], axis=0, keepdims=True)
    line = lax.broadcasted_iota(jnp.int32, (16, pairs), 0)
    parts = channels // pairs
    rows = small_ref.shape[0] // parts
    for n in range(parts):
        here = slice(n * pairs, (n + 1) * pairs)
        small_ref[n * rows : n * rows + 2 * hidden, :] = weights[:, here]
        small_ref[n * rows + 2 * hidden : (n + 1) * rows, :] = jnp.where(
            line == 0,
            gain_part[:, here],
            jnp.where(line == 1, bias_ref[:1, :], jnp.zeros((16, pairs), f32)),
        )


def share_kernel(res, diag_ref, spread_ref, out_ref, outs):
    hidden = diag_ref.shape[0] // 2
    pairs = out_ref.shape[1]
    seqs = diag_ref.shape[1] // (2 * res)
    grad = mm_t(diag_ref[...], spread_ref[...]) * (1.0 / seqs)
    for d in range(hidden):
        at = (d % 2) * hidden
        outs[d * (hidden + 1) : d * (hidden + 1) + hidden, :] = grad[
            at : at + hidden, (d // 2) * pairs : (d // 2 + 1) * pairs
        ]
    index = lax.axis_index("row")
    for place in range(hidden):
        chunk = lax.bitwise_xor(index, place % 4 * 8 + place // 4 % 4 * 2 + place // 16)
        out_ref[place * hidden : (place + 1) * hidden, :] = outs[
            pl.ds(chunk, hidden, stride=hidden + 1), :
        ]


def result_kernel(
    rights_ref, twin_left_ref, w1_ref, normed_ref, bias_ref, normed_grad_ref, scaled_ref, recip_ref, gain_ref,
    delta_ref, grad_ref,
    rows, mixed,
):
    res, _, pairs = delta_ref.shape
    seqs = grad_ref.shape[0]
    hidden = w1_ref.shape[0]
    left = mm_t(normed_ref[...], w1_ref[...]).astype(bf16)
    for d in range(hidden):
        at = (d % 2) * hidden
        part = mm(left, twin_left_ref[at : at + hidden, (d // 2) * pairs : (d // 2 + 1) * pairs])
        part = part.astype(bf16)
        for r in range(res):
            mixed[d * seqs : (d + 1) * seqs, r * pairs : (r + 1) * pairs] = part[
                r * seqs : (r + 1) * seqs, :
            ]
    delta = mm(rights_ref[...], mixed[...]) * (1.0 / seqs)
    for r in range(res):
        delta_ref[r] = (delta[:, r * pairs : (r + 1) * pairs] + bias_ref[...]).astype(bf16)
    scaled = scaled_ref[...]
    scaled_grad = normed_grad_ref[...] * gain_ref[...]
    centre = jnp.mean(scaled_grad, axis=-1, keepdims=True)
    slope = jnp.mean(scaled_grad * scaled, axis=-1, keepdims=True)
    grad = recip_ref[:, :1] * (scaled_grad - centre - scaled * slope)
    for r in range(res):
        rows[:, r, :] = grad[r * seqs : (r + 1) * seqs, :]
    grad_ref[...] = rows[...].astype(bf16)


def split(small, out, small_ref, out_ref, sends):
    small = small.astype(bf16)
    rows = out_ref.shape[0]
    small_ref[...] = small
    out_ref[...] = out[:rows]
    for k, send in enumerate(sends):
        send[: small.shape[0], :] = small
        send[small.shape[0] :, :] = out[(k + 1) * rows : (k + 2) * rows].astype(bf16)


def total(small_ref, out_ref, came):
    height = small_ref.shape[0]
    one, two, three = (c[:height, :].astype(f32) for c in came)
    small = (small_ref[...].astype(f32) + one) + (two + three)
    one, two, three = (c[height:, :].astype(f32) for c in came)
    return small, (out_ref[...] + one) + (two + three)


def join_kernel(small_in, small_came, out_in, out_came, small_ref, out_ref, *sends):
    kept = out_in[: out_came.shape[0], :] + out_came[...].astype(f32)
    split(small_in[...] + small_came[...], kept, small_ref, out_ref, sends)


def merge_kernel(small_in, out_in, one, two, three, small_ref, out_ref, *sends):
    small, out = total(small_in, out_in, (one, two, three))
    split(small, out, small_ref, out_ref, sends)


def finish_kernel(
    scale, small_in, out_in, one, two, three,
    gain_hbm, left_hbm, right_hbm, out_hbm, bias_hbm,
    whole, out_ref, sems,
):
    hidden = left_hbm.shape[0]
    pairs = bias_hbm.shape[1]
    small, out = total(small_in, out_in, (one, two, three))
    rows = whole.shape[0]
    for n in range(whole.shape[1] // pairs):
        whole[:, n * pairs : (n + 1) * pairs] = small[n * rows : (n + 1) * rows] * scale
    out_ref[...] = out * scale
    copies = fetch(
        [
            (whole.at[2 * hidden : 2 * hidden + 1, :], gain_hbm),
            (whole.at[:hidden, :], left_hbm),
            (whole.at[hidden : 2 * hidden, :], right_hbm),
            (out_ref, out_hbm),
            (whole.at[2 * hidden + 1 : 2 * hidden + 2, :pairs], bias_hbm),
        ],
        sems,
    )
    for copy in copies:
        copy.wait()


def call(kernel, name, args, outs, scratch, flops, remote_in=False, remote_out=False, vmem=16):
    moved = sum(a.size * a.dtype.itemsize for a in args)
    space = lambda far: pl.BlockSpec(memory_space=pltpu.HBM if far else pltpu.VMEM)
    sems = max(len(args) * remote_in, len(outs) * remote_out)
    shapes = [pltpu.VMEM(s, d) for s, d in scratch]
    if sems:
        shapes.append(pltpu.SemaphoreType.DMA((sems,)))
    return pl.pallas_call(
        kernel,
        out_shape=[jax.ShapeDtypeStruct(s, d) for s, d in outs],
        in_specs=[space(remote_in)] * len(args),
        out_specs=[space(remote_out)] * len(outs),
        scratch_shapes=shapes,
        compiler_params=pltpu.CompilerParams(vmem_limit_bytes=vmem * 1024 * 1024),
        cost_estimate=pl.CostEstimate(flops=flops, bytes_accessed=moved, transcendentals=0),
        name=name,
    )(*args)


def swap(value, step):
    count = lax.axis_size("row")
    return lax.ppermute(value, "row", [(i, i ^ step) for i in range(count)])


def on_device_row(
    homolog_features,
    standardize_multiplier,
    first_factor_weights,
    second_factor_weights,
    output_projection_matrix,
    output_bias,
    pair_cotangent,
):
    seqs, res, channels = homolog_features.shape
    hidden = first_factor_weights.shape[1]
    pairs = output_projection_matrix.shape[1]
    count = lax.axis_size("row")
    columns = res * count
    own = seqs * res
    lanes = 2 * seqs
    twins = hidden // 2
    gain = standardize_multiplier.reshape(1, channels)
    bias = output_bias.reshape(1, pairs)
    w1, w2 = first_factor_weights.T, second_factor_weights.T
    wide = (2 * hidden, twins * pairs)

    zs, yxs = 4, 4
    height = res * hidden
    *sends, scaled, normed, recip, diag = call(
        factor_kernel,
        "factors",
        (homolog_features, gain, w1, w2, pair_cotangent),
        [
            *[((height + res * columns // zs, lanes), bf16)] * zs,
            ((own, channels), f32),
            ((own, channels), bf16),
            ((own, 128), f32),
            ((2 * hidden, res * lanes), bf16),
        ],
        [
            ((seqs, res, channels), bf16),
            ((1, channels), f32),
            ((hidden, channels), bf16),
            ((hidden, channels), bf16),
            ((res, columns, pairs), bf16),
            ((seqs, res, channels), f32),
            ((res, 2 * hidden, lanes), f32),
            ((res * columns, pairs), f32),
            ((res * res * (count + 1), pairs), f32),
        ],
        10**6,
        remote_in=True,
        vmem=60,
    )
    swapped = {z: swap(sends[z], z * 2 * yxs) for z in (3, 2, 1)}
    own_send, normed = call(
        own_kernel,
        "own",
        (sends[0], normed),
        [(sends[0].shape, bf16), (normed.shape, bf16)],
        [],
        10**6,
    )
    sent = call(
        functools.partial(pack_kernel, height),
        "pack",
        [own_send] + [swapped[z] for z in range(1, zs)],
        [((zs * height + zs * 2 * res * res, lanes), bf16)] * yxs,
        [],
        10**6,
    )
    mine = [sent[0]] + [swap(sent[yx], yx * 2) for yx in range(1, yxs)]
    prepared = call(
        prepare_kernel,
        "prepare",
        (output_projection_matrix, pair_cotangent, scaled, w1, w2),
        [
            ((res * pairs, columns), bf16),
            (wide, bf16),
            (wide, bf16),
            ((8, pairs), f32),
            (scaled.shape, f32),
            (w1.shape, bf16),
            (w2.shape, bf16),
        ],
        [((hidden * hidden, pairs), f32)],
        10**6,
    )
    mine[0], prepared = lax.optimization_barrier((mine[0], prepared))
    cot_t, twin_left, twin_right, bias_part, scaled, w1, w2 = prepared
    other = [swap(m, 1) for m in mine]
    small, rights, spread, normed_grad = call(
        functools.partial(sums_kernel, yxs),
        "sums",
        (
            cot_t, twin_left, twin_right, normed, scaled, w1, w2, bias_part, *mine, *other,
        ),
        [
            ((channels // pairs * (2 * hidden + 16), pairs), f32),
            ((columns, hidden * seqs), bf16),
            ((twins * pairs, res * lanes), bf16),
            ((own, channels), f32),
        ],
        [
            (((columns + 1) * hidden, lanes), f32),
            ((columns, hidden * seqs), bf16),
            ((twins * pairs, res * lanes), bf16),
            ((res * columns, pairs), f32),
            ((res * pairs, columns), bf16),
        ],
        10**6,
    )
    (out_part,) = call(
        functools.partial(share_kernel, res),
        "shares",
        (diag, spread),
        [((hidden * hidden, pairs), f32)],
        [((hidden * (hidden + 1), pairs), f32)],
        10**6,
    )
    delta, grad = call(
        result_kernel,
        "results",
        (rights, twin_left, w1, normed, bias, normed_grad, scaled, recip, gain),
        [((res, columns, pairs), bf16), ((seqs, res, channels), bf16)],
        [((seqs, res, channels), f32), ((hidden * seqs, res * pairs), bf16)],
        10**6,
    )
    height = small.shape[0]
    half = hidden * hidden // 2

    def step(kernel, name, args, rows):
        kept, out, *sends = call(
            kernel,
            name,
            args,
            [((height, pairs), bf16), ((rows, pairs), f32)] + [((height + rows, pairs), bf16)] * 3,
            [],
            10**6,
        )
        return kept, out, sends

    out_came = swap(out_part[half:].astype(bf16), 1)
    kept, out, sends = step(
        join_kernel, "join", (small, swap(small, 1), out_part, out_came), half // yxs
    )
    came = {k: swap(sends[k - 1], k * 2) for k in (3, 1, 2)}
    kept, delta, grad = lax.optimization_barrier((kept, delta, grad))
    kept, out, sends = step(merge_kernel, "merge", (kept, out, came[1], came[2], came[3]), half // yxs // zs)
    came = {k: swap(sends[k - 1], k * 2 * yxs) for k in (3, 2, 1)}
    gain_out, left_out, right_out, out_share, bias_out = call(
        functools.partial(finish_kernel, 1.0 / columns),
        "finish",
        (kept, out, came[1], came[2], came[3]),
        [
            ((1, channels), f32),
            ((hidden, channels), f32),
            ((hidden, channels), f32),
            ((hidden * hidden // count, pairs), f32),
            ((1, pairs), f32),
        ],
        [((2 * hidden + 16, channels), f32), ((hidden * hidden // count, pairs), f32)],
        10**6,
        remote_out=True,
    )
    return (
        delta,
        grad,
        gain_out.reshape(channels),
        left_out.T,
        right_out.T,
        out_share,
        bias_out.reshape(pairs),
    )


def solution(mesh):
    in_specs = (P(None, ("col", "row"), None), P(), P(), P(), P(), P(), P("row", "col", None))
    out_specs = (
        P("row", "col", None),
        P(None, ("col", "row"), None),
        P(),
        P(),
        P(),
        P(("row", "col"), None),
        P(),
    )
    one_row = mesh.shape["row"] == 32 and mesh.shape["col"] == 1
    body = on_device_row if one_row else on_device
    return jax.shard_map(
        body, mesh=mesh, in_specs=in_specs, out_specs=out_specs, check_vma=False
    )
```

```python
import functools
import math

import jax
import jax.numpy as jnp
from jax import lax
from jax.experimental import pallas as pl
from jax.experimental.pallas import tpu as pltpu
from jax.sharding import PartitionSpec as P

ln_epsilon = 1e-05


def from_root(value, axis, root):
    mine = lax.axis_index(axis) == root
    return lax.psum(jnp.where(mine, value, jnp.zeros_like(value)), axis)


def layer_norm_output(homolog_features, standardize_multiplier):
    value_entries = homolog_features.astype(jnp.float32)
    centred = value_entries - jnp.mean(value_entries, axis=-1, keepdims=True)
    reciprocal_deviation = lax.rsqrt(
        jnp.mean(centred * centred, axis=-1, keepdims=True) + ln_epsilon
    )
    scaled_rows = centred * reciprocal_deviation
    normalized_rows = (scaled_rows * standardize_multiplier).astype(jnp.bfloat16)
    return (scaled_rows, reciprocal_deviation, normalized_rows)


def on_device(
    homolog_features,
    standardize_multiplier,
    first_factor_weights,
    second_factor_weights,
    output_projection_matrix,
    output_bias,
    pair_cotangent,
):
    sequence_count, local_residues, channel_count = homolog_features.shape
    hidden = first_factor_weights.shape[1]
    pair_channels = output_projection_matrix.shape[1]
    row_count = lax.axis_size("row")
    col_count = lax.axis_size("col")
    ratio = row_count // col_count
    row_index = lax.axis_index("row")
    col_index = lax.axis_index("col")
    scaled_rows, reciprocal_deviation, normalized_rows = layer_norm_output(
        homolog_features, standardize_multiplier
    )
    left_own = jnp.dot(
        normalized_rows, first_factor_weights, preferred_element_type=jnp.float32
    ).astype(jnp.bfloat16)
    right_own = jnp.dot(
        normalized_rows, second_factor_weights, preferred_element_type=jnp.float32
    ).astype(jnp.bfloat16)
    left_cols, right_cols = (
        lax.all_gather(
            left_own.reshape(sequence_count, local_residues * hidden), "row", axis=1, tiled=True
        ),
        lax.all_gather(
            right_own.reshape(sequence_count, local_residues * hidden), "row", axis=1, tiled=True
        ),
    )
    col_res = local_residues * row_count
    row_res = col_res // ratio
    offset = row_index % ratio * row_res
    piece_flat = lax.dynamic_slice_in_dim(left_cols, offset * hidden, row_res * hidden, 1)
    left_rows = from_root(piece_flat, "col", row_index // ratio).reshape(
        sequence_count, row_res, hidden
    )
    right_block = right_cols.reshape(sequence_count, col_res, hidden)
    group = math.gcd(row_res, max(1, 512 // col_res))
    blocks = row_res // group
    left_steps = jnp.transpose(
        left_rows.reshape(sequence_count, blocks, group, hidden), (1, 0, 2, 3)
    )
    grad_steps = pair_cotangent.reshape(blocks, group, col_res, pair_channels)
    per_homolog_weight = 1.0 / sequence_count

    def pair_step(carried, inputs):
        out_acc, right_acc = carried
        left_blk, grad_blk = inputs
        outer = (
            jnp.einsum("sic,sjd->ijcd", left_blk, right_block, preferred_element_type=jnp.float32)
            * per_homolog_weight
        )
        outer_bf = outer.reshape(group * col_res, hidden * hidden).astype(jnp.bfloat16)
        update = (
            jnp.dot(outer_bf, output_projection_matrix, preferred_element_type=jnp.float32)
            + output_bias
        ).astype(jnp.bfloat16)
        grad_rows = grad_blk.reshape(group * col_res, pair_channels)
        out_acc = out_acc + lax.dot_general(
            outer_bf, grad_rows, (((0,), (0,)), ((), ())), preferred_element_type=jnp.float32
        )
        outer_grad = jnp.dot(
            grad_rows, output_projection_matrix.T, preferred_element_type=jnp.float32
        ).astype(jnp.bfloat16)
        outer_grad = outer_grad.reshape(group, col_res, hidden, hidden)
        left_blk_grad = (
            jnp.einsum("ijcd,sjd->sic", outer_grad, right_block, preferred_element_type=jnp.float32)
            * per_homolog_weight
        )
        right_acc = (
            right_acc
            + jnp.einsum("ijcd,sic->sjd", outer_grad, left_blk, preferred_element_type=jnp.float32)
            * per_homolog_weight
        )
        return (
            (out_acc, right_acc),
            (update.reshape(group, col_res, pair_channels), left_blk_grad),
        )

    initial_carry = (
        jnp.zeros((hidden * hidden, pair_channels), jnp.float32),
        jnp.zeros((sequence_count, col_res, hidden), jnp.float32),
    )
    (out_acc, right_part), (updates, first_factor_pieces) = lax.scan(
        pair_step, initial_carry, (left_steps, grad_steps)
    )
    pair_delta = updates.reshape(row_res, col_res, pair_channels)
    left_part = jnp.transpose(first_factor_pieces, (1, 0, 2, 3)).reshape(
        sequence_count, row_res * hidden
    )
    right_flat = right_part.reshape(sequence_count, col_res * hidden)
    left_row = lax.psum(left_part, "col")
    owner = row_index // ratio == col_index
    slotted = lax.dynamic_update_slice_in_dim(
        jnp.zeros((sequence_count, col_res * hidden), jnp.float32),
        jnp.where(owner, left_row, 0.0),
        offset * hidden,
        1,
    )
    first_factor_total, right_sum = (
        lax.psum_scatter(slotted, "row", scatter_dimension=1, tiled=True),
        lax.psum_scatter(right_flat, "row", scatter_dimension=1, tiled=True),
    )
    left_bf = first_factor_total.reshape(sequence_count, local_residues, hidden).astype(
        jnp.bfloat16
    )
    right_bf = right_sum.reshape(sequence_count, local_residues, hidden).astype(jnp.bfloat16)
    normed_grad = jnp.dot(
        left_bf, first_factor_weights.T, preferred_element_type=jnp.float32
    ) + jnp.dot(right_bf, second_factor_weights.T, preferred_element_type=jnp.float32)
    scaled_gradient = normed_grad * standardize_multiplier
    centering_term = jnp.mean(scaled_gradient, axis=-1, keepdims=True)
    gradient_slope_term = jnp.mean(scaled_gradient * scaled_rows, axis=-1, keepdims=True)
    alignment_gradient = (
        reciprocal_deviation
        * (scaled_gradient - centering_term - scaled_rows * gradient_slope_term)
    ).astype(jnp.bfloat16)
    gain_part = jnp.sum(normed_grad * scaled_rows, axis=(0, 1))
    left_weight = jnp.einsum(
        "srm,srh->mh", normalized_rows, left_bf, preferred_element_type=jnp.float32
    )
    right_weight = jnp.einsum(
        "srm,srh->mh", normalized_rows, right_bf, preferred_element_type=jnp.float32
    )
    bias_part = jnp.sum(pair_cotangent, axis=(0, 1), dtype=jnp.float32)
    left_total, right_total, gain_total, bias_total = lax.psum(
        (left_weight, right_weight, gain_part, bias_part), ("row", "col")
    )
    out_share = lax.psum_scatter(out_acc, ("row", "col"), scatter_dimension=0, tiled=True)
    scale = 1.0 / (local_residues * row_count * col_count)
    return (
        pair_delta,
        alignment_gradient,
        gain_total * scale,
        left_total * scale,
        right_total * scale,
        out_share * scale,
        bias_total * scale,
    )


f32 = jnp.float32
bf16 = jnp.bfloat16


def mm(a, b):
    return lax.dot_general(a, b, (((1,), (0,)), ((), ())), preferred_element_type=f32)


def mm_t(a, b):
    return lax.dot_general(a, b, (((1,), (1,)), ((), ())), preferred_element_type=f32)


def fetch(pairs, sems):
    copies = [pltpu.make_async_copy(a, b, sems.at[n]) for n, (a, b) in enumerate(pairs)]
    for copy in copies:
        copy.start()
    return copies


def normalise(x):
    centred = x - jnp.mean(x, axis=-1, keepdims=True)
    recip = lax.rsqrt(jnp.mean(centred * centred, axis=-1, keepdims=True) + ln_epsilon)
    return centred * recip, recip


def factor_kernel(
    x_hbm, gain_hbm, w1_hbm, w2_hbm, cot_hbm,
    send0_ref, send1_ref, send2_ref, send3_ref,
    x_ref, gain_ref, w1_ref, w2_ref, cot_ref, rows, twin, cots, moved, sems,
):
    copies = fetch(
        [(x_hbm, x_ref), (gain_hbm, gain_ref), (w1_hbm, w1_ref), (w2_hbm, w2_ref), (cot_hbm, cot_ref)],
        sems,
    )
    sends = (send0_ref, send1_ref, send2_ref, send3_ref)
    seqs, res, _ = x_ref.shape
    hidden = w1_ref.shape[0]
    columns = cot_ref.shape[1]
    devices = columns // res
    copies[0].wait()
    rows[...] = x_ref[...].astype(f32)
    for copy in copies[1:]:
        copy.wait()
    both = jnp.concatenate([w1_ref[...], w2_ref[...]], axis=0)
    low = lax.broadcasted_iota(jnp.int32, (hidden, 2 * seqs), 1) < seqs
    for r in range(res):
        scaled, _ = normalise(rows[:, r, :])
        normed = (scaled * gain_ref[...]).astype(bf16)
        twin[r] = mm_t(both, jnp.concatenate([normed, normed], axis=0))
        even = twin[r, pl.ds(0, hidden, stride=2), :]
        odd = twin[r, pl.ds(1, hidden, stride=2), :]
        piece = jnp.where(low, even, odd).astype(bf16)
        for send_ref in sends:
            send_ref[r * hidden : (r + 1) * hidden, :] = piece
    for r in range(res):
        cots[r * columns : (r + 1) * columns, :] = cot_ref[r].astype(f32)
    for r in range(res):
        for q in range(res):
            block = cots[pl.ds(r * columns + q, devices, stride=res), :]
            at = (r * res + q) * (devices + 1)
            moved[at : at + devices, :] = block
    index = lax.axis_index("row")
    per = res * res
    plane = devices // len(sends)
    for n in range(devices):
        block = moved[pl.ds(lax.bitwise_xor(index, n), per, stride=devices + 1), :]
        to = res * hidden + n % plane * per
        sends[n // plane][to : to + per, :] = block.astype(bf16)


def copy_kernel(*refs):
    for a, b in zip(refs[: len(refs) // 2], refs[len(refs) // 2 :]):
        b[...] = a[...]


def own_kernel(
    send_in, x_ref, gain_ref, w1_ref,
    send_ref, scaled_ref, normed_ref, recip_ref, diag_ref,
    rows,
):
    send_ref[...] = send_in[...]
    seqs, res, _ = x_ref.shape
    hidden = w1_ref.shape[0]
    rows[...] = x_ref[...].astype(f32)
    low = lax.broadcasted_iota(jnp.int32, (hidden, 2 * seqs), 1) < seqs
    for r in range(res):
        scaled, recip = normalise(rows[:, r, :])
        at = slice(r * seqs, (r + 1) * seqs)
        scaled_ref[at, :] = scaled
        recip_ref[at, :] = jnp.broadcast_to(recip, (seqs, recip_ref.shape[1]))
        normed = (scaled * gain_ref[...]).astype(bf16)
        normed_ref[at, :] = normed
        left = mm_t(w1_ref[...], jnp.concatenate([normed, normed], axis=0))
        zero = jnp.zeros_like(left)
        lanes = slice(r * 2 * seqs, (r + 1) * 2 * seqs)
        diag_ref[:hidden, lanes] = jnp.where(low, left, zero).astype(bf16)
        diag_ref[hidden:, lanes] = jnp.where(low, zero, left).astype(bf16)


def pack_kernel(height, *refs):
    held, sent = refs[: len(refs) // 2], refs[len(refs) // 2 :]
    cut = (held[0].shape[0] - height) // len(sent)
    for z, h in enumerate(held):
        factors = h[:height, :]
        for yx, s in enumerate(sent):
            s[z * height : (z + 1) * height, :] = factors
            to = len(held) * height + z * cut
            s[to : to + cut, :] = h[height + yx * cut : height + (yx + 1) * cut, :]


def prepare_kernel(
    out_w_ref, cot_ref, w1_in, w2_in,
    cot_t_ref, twin_left_ref, twin_right_ref, bias_ref, w1_ref, w2_ref,
    wide,
):
    hidden = twin_left_ref.shape[0] // 2
    res, columns, pairs = cot_ref.shape
    copy_kernel(w1_in, w2_in, w1_ref, w2_ref)
    wide[...] = out_w_ref[...].astype(f32)
    for d in range(hidden):
        at = (d % 2) * hidden
        twin_left_ref[at : at + hidden, (d // 2) * pairs : (d // 2 + 1) * pairs] = wide[
            pl.ds(d, hidden, stride=hidden), :
        ].astype(bf16)
    for q in range(hidden // 2):
        twin_right_ref[:, q * pairs : (q + 1) * pairs] = out_w_ref[
            q * 2 * hidden : (q + 1) * 2 * hidden, :
        ]
    total = jnp.zeros((1, pairs), f32)
    for r in range(res):
        cot = cot_ref[r].astype(f32)
        total = total + jnp.sum(cot, axis=0, keepdims=True)
        cot_t_ref[r * pairs : (r + 1) * pairs, :] = cot.T.astype(bf16)
    bias_ref[...] = jnp.broadcast_to(total, bias_ref.shape)


def sums_kernel(
    yxs, cot_t_ref, twin_left_ref, twin_right_ref, normed_ref, scaled_ref,
    w1_ref, w2_ref, bias_ref, *refs,
):
    mine, other = refs[:yxs], refs[yxs : 2 * yxs]
    small_ref, rights_ref, spread_ref, grad_ref, wide, lefts, turned, cots, got_t = refs[2 * yxs :]
    columns = rights_ref.shape[0]
    lanes = mine[0].shape[1]
    seqs = lanes // 2
    channels = normed_ref.shape[1]
    hidden = w1_ref.shape[0]
    twins = hidden // 2
    pairs = bias_ref.shape[1]
    res = spread_ref.shape[1] // lanes
    index = lax.axis_index("row")
    height = res * hidden
    per = res * res
    zs = columns // (2 * yxs * res)
    for yx in range(yxs):
        for z in range(zs):
            factors = slice(z * height, (z + 1) * height)
            first = zs * height + z * 2 * per
            for core, ref in enumerate((mine[yx], other[yx])):
                device = lax.bitwise_xor(index, z * 2 * yxs + yx * 2 + core)
                block = ref[factors, :].astype(f32)
                for r in range(res):
                    wide[pl.ds(device * res + r, hidden, stride=columns + 1), :] = block[
                        r * hidden : (r + 1) * hidden
                    ]
                block = ref[first + core * per : first + (core + 1) * per, :]
                at = pl.multiple_of(device * per, per)
                cots[pl.ds(at, per), :] = block.astype(f32)
    for r in range(res):
        got_t[r * pairs : (r + 1) * pairs, :] = cots[pl.ds(r, columns, stride=res), :].T.astype(bf16)
    for q in range(twins):
        here = slice(q * lanes, (q + 1) * lanes)
        at = q * (columns + 1)
        lefts[:, here] = wide[at : at + columns, :].astype(bf16)
        at = (twins + q) * (columns + 1)
        rights_ref[:, here] = wide[at : at + columns, :].astype(bf16)

    def summed(cots, factors, weights, out):
        for q in range(0, twins, 2):
            block = mm(cots[...], factors[:, q * lanes : (q + 2) * lanes]).astype(bf16)
            for r in range(res):
                for e in range(2):
                    out[(q + e) * pairs : (q + e + 1) * pairs, r * lanes : (r + 1) * lanes] = block[
                        r * pairs : (r + 1) * pairs, e * lanes : (e + 1) * lanes
                    ]
        t = mm(weights[...], out[...]).T
        parts = [
            t[r * lanes : r * lanes + seqs, :hidden] + t[r * lanes + seqs : (r + 1) * lanes, hidden:]
            for r in range(res)
        ]
        return jnp.concatenate(parts, axis=0) * (1.0 / seqs)

    left_sum = summed(cot_t_ref, rights_ref, twin_left_ref, spread_ref)
    right_sum = summed(got_t, lefts, twin_right_ref, turned)
    normed_grad = mm(left_sum.astype(bf16), w1_ref[...]) + mm(right_sum.astype(bf16), w2_ref[...])
    grad_ref[...] = normed_grad
    factors_t = jnp.concatenate([left_sum, right_sum], axis=1).T.astype(bf16)
    weights = mm(factors_t, normed_ref[...])
    gain_part = jnp.sum(normed_grad * scaled_ref[...], axis=0, keepdims=True)
    line = lax.broadcasted_iota(jnp.int32, (16, pairs), 0)
    parts = channels // pairs
    rows = small_ref.shape[0] // parts
    for n in range(parts):
        here = slice(n * pairs, (n + 1) * pairs)
        small_ref[n * rows : n * rows + 2 * hidden, :] = weights[:, here]
        small_ref[n * rows + 2 * hidden : (n + 1) * rows, :] = jnp.where(
            line == 0,
            gain_part[:, here],
            jnp.where(line == 1, bias_ref[:1, :], jnp.zeros((16, pairs), f32)),
        )


def share_kernel(res, diag_ref, spread_ref, out_ref, outs):
    hidden = diag_ref.shape[0] // 2
    pairs = out_ref.shape[1]
    seqs = diag_ref.shape[1] // (2 * res)
    grad = mm_t(diag_ref[...], spread_ref[...]) * (1.0 / seqs)
    for d in range(hidden):
        at = (d % 2) * hidden
        outs[d * (hidden + 1) : d * (hidden + 1) + hidden, :] = grad[
            at : at + hidden, (d // 2) * pairs : (d // 2 + 1) * pairs
        ]
    index = lax.axis_index("row")
    for place in range(hidden):
        chunk = lax.bitwise_xor(index, place % 4 * 8 + place // 4 % 4 * 2 + place // 16)
        out_ref[place * hidden : (place + 1) * hidden, :] = outs[
            pl.ds(chunk, hidden, stride=hidden + 1), :
        ]


def result_kernel(
    rights_ref, twin_left_ref, w1_ref, normed_ref, bias_ref, normed_grad_ref, scaled_ref, recip_ref, gain_ref,
    delta_ref, grad_ref,
    rows, mixed,
):
    res, _, pairs = delta_ref.shape
    seqs = grad_ref.shape[0]
    hidden = w1_ref.shape[0]
    left = mm_t(normed_ref[...], w1_ref[...]).astype(bf16)
    for d in range(hidden):
        at = (d % 2) * hidden
        part = mm(left, twin_left_ref[at : at + hidden, (d // 2) * pairs : (d // 2 + 1) * pairs])
        part = part.astype(bf16)
        for r in range(res):
            mixed[d * seqs : (d + 1) * seqs, r * pairs : (r + 1) * pairs] = part[
                r * seqs : (r + 1) * seqs, :
            ]
    delta = mm(rights_ref[...], mixed[...]) * (1.0 / seqs)
    for r in range(res):
        delta_ref[r] = (delta[:, r * pairs : (r + 1) * pairs] + bias_ref[...]).astype(bf16)
    scaled = scaled_ref[...]
    scaled_grad = normed_grad_ref[...] * gain_ref[...]
    centre = jnp.mean(scaled_grad, axis=-1, keepdims=True)
    slope = jnp.mean(scaled_grad * scaled, axis=-1, keepdims=True)
    grad = recip_ref[:, :1] * (scaled_grad - centre - scaled * slope)
    for r in range(res):
        rows[:, r, :] = grad[r * seqs : (r + 1) * seqs, :]
    grad_ref[...] = rows[...].astype(bf16)


def split(small, out, small_ref, out_ref, sends):
    small = small.astype(bf16)
    rows = out_ref.shape[0]
    small_ref[...] = small
    out_ref[...] = out[:rows]
    for k, send in enumerate(sends):
        send[: small.shape[0], :] = small
        send[small.shape[0] :, :] = out[(k + 1) * rows : (k + 2) * rows].astype(bf16)


def total(small_ref, out_ref, came):
    height = small_ref.shape[0]
    one, two, three = (c[:height, :].astype(f32) for c in came)
    small = (small_ref[...].astype(f32) + one) + (two + three)
    one, two, three = (c[height:, :].astype(f32) for c in came)
    return small, (out_ref[...] + one) + (two + three)


def join_kernel(small_in, small_came, out_in, out_came, small_ref, out_ref, *sends):
    kept = out_in[: out_came.shape[0], :] + out_came[...].astype(f32)
    split(small_in[...] + small_came[...], kept, small_ref, out_ref, sends)


def merge_kernel(small_in, out_in, one, two, three, small_ref, out_ref, *sends):
    small, out = total(small_in, out_in, (one, two, three))
    split(small, out, small_ref, out_ref, sends)


def finish_kernel(
    scale, small_in, out_in, one, two, three,
    gain_hbm, left_hbm, right_hbm, out_hbm, bias_hbm,
    whole, out_ref, sems,
):
    hidden = left_hbm.shape[0]
    pairs = bias_hbm.shape[1]
    small, out = total(small_in, out_in, (one, two, three))
    rows = whole.shape[0]
    for n in range(whole.shape[1] // pairs):
        whole[:, n * pairs : (n + 1) * pairs] = small[n * rows : (n + 1) * rows] * scale
    out_ref[...] = out * scale
    copies = fetch(
        [
            (whole.at[2 * hidden : 2 * hidden + 1, :], gain_hbm),
            (whole.at[:hidden, :], left_hbm),
            (whole.at[hidden : 2 * hidden, :], right_hbm),
            (out_ref, out_hbm),
            (whole.at[2 * hidden + 1 : 2 * hidden + 2, :pairs], bias_hbm),
        ],
        sems,
    )
    for copy in copies:
        copy.wait()


def call(kernel, name, args, outs, scratch, flops, remote_in=False, remote_out=False, vmem=16):
    moved = sum(a.size * a.dtype.itemsize for a in args)
    space = lambda far: pl.BlockSpec(memory_space=pltpu.HBM if far else pltpu.VMEM)
    sems = max(len(args) * remote_in, len(outs) * remote_out)
    shapes = [pltpu.VMEM(s, d) for s, d in scratch]
    if sems:
        shapes.append(pltpu.SemaphoreType.DMA((sems,)))
    return pl.pallas_call(
        kernel,
        out_shape=[jax.ShapeDtypeStruct(s, d) for s, d in outs],
        in_specs=[space(remote_in)] * len(args),
        out_specs=[space(remote_out)] * len(outs),
        scratch_shapes=shapes,
        compiler_params=pltpu.CompilerParams(vmem_limit_bytes=vmem * 1024 * 1024),
        cost_estimate=pl.CostEstimate(flops=flops, bytes_accessed=moved, transcendentals=0),
        name=name,
    )(*args)


def swap(value, step):
    count = lax.axis_size("row")
    return lax.ppermute(value, "row", [(i, i ^ step) for i in range(count)])


def on_device_row(
    homolog_features,
    standardize_multiplier,
    first_factor_weights,
    second_factor_weights,
    output_projection_matrix,
    output_bias,
    pair_cotangent,
):
    seqs, res, channels = homolog_features.shape
    hidden = first_factor_weights.shape[1]
    pairs = output_projection_matrix.shape[1]
    count = lax.axis_size("row")
    columns = res * count
    own = seqs * res
    lanes = 2 * seqs
    twins = hidden // 2
    gain = standardize_multiplier.reshape(1, channels)
    bias = output_bias.reshape(1, pairs)
    w1, w2 = first_factor_weights.T, second_factor_weights.T
    wide = (2 * hidden, twins * pairs)

    zs, yxs = 4, 4
    height = res * hidden
    sends = call(
        factor_kernel,
        "factors",
        (homolog_features, gain, w1, w2, pair_cotangent),
        [
            *[((height + res * columns // zs, lanes), bf16)] * zs,
        ],
        [
            ((seqs, res, channels), bf16),
            ((1, channels), f32),
            ((hidden, channels), bf16),
            ((hidden, channels), bf16),
            ((res, columns, pairs), bf16),
            ((seqs, res, channels), f32),
            ((res, 2 * hidden, lanes), f32),
            ((res * columns, pairs), f32),
            ((res * res * (count + 1), pairs), f32),
        ],
        10**6,
        remote_in=True,
        vmem=60,
    )
    swapped = {z: swap(sends[z], z * 2 * yxs) for z in (3, 2, 1)}
    own_send, scaled, normed, recip, diag = call(
        own_kernel,
        "own",
        (sends[0], homolog_features, gain, w1),
        [
            (sends[0].shape, bf16),
            ((own, channels), f32),
            ((own, channels), bf16),
            ((own, 128), f32),
            ((2 * hidden, res * lanes), bf16),
        ],
        [((seqs, res, channels), f32)],
        10**6,
    )
    sent = call(
        functools.partial(pack_kernel, height),
        "pack",
        [own_send] + [swapped[z] for z in range(1, zs)],
        [((zs * height + zs * 2 * res * res, lanes), bf16)] * yxs,
        [],
        10**6,
    )
    mine = [sent[0]] + [swap(sent[yx], yx * 2) for yx in range(1, yxs)]
    prepared = call(
        prepare_kernel,
        "prepare",
        (output_projection_matrix, pair_cotangent, w1, w2),
        [
            ((res * pairs, columns), bf16),
            (wide, bf16),
            (wide, bf16),
            ((8, pairs), f32),
            (w1.shape, bf16),
            (w2.shape, bf16),
        ],
        [((hidden * hidden, pairs), f32)],
        10**6,
    )
    mine[0], prepared = lax.optimization_barrier((mine[0], prepared))
    cot_t, twin_left, twin_right, bias_part, w1, w2 = prepared
    other = [swap(m, 1) for m in mine]
    small, rights, spread, normed_grad = call(
        functools.partial(sums_kernel, yxs),
        "sums",
        (
            cot_t, twin_left, twin_right, normed, scaled, w1, w2, bias_part, *mine, *other,
        ),
        [
            ((channels // pairs * (2 * hidden + 16), pairs), f32),
            ((columns, hidden * seqs), bf16),
            ((twins * pairs, res * lanes), bf16),
            ((own, channels), f32),
        ],
        [
            (((columns + 1) * hidden, lanes), f32),
            ((columns, hidden * seqs), bf16),
            ((twins * pairs, res * lanes), bf16),
            ((res * columns, pairs), f32),
            ((res * pairs, columns), bf16),
        ],
        10**6,
    )
    (out_part,) = call(
        functools.partial(share_kernel, res),
        "shares",
        (diag, spread),
        [((hidden * hidden, pairs), f32)],
        [((hidden * (hidden + 1), pairs), f32)],
        10**6,
    )
    delta, grad = call(
        result_kernel,
        "results",
        (rights, twin_left, w1, normed, bias, normed_grad, scaled, recip, gain),
        [((res, columns, pairs), bf16), ((seqs, res, channels), bf16)],
        [((seqs, res, channels), f32), ((hidden * seqs, res * pairs), bf16)],
        10**6,
    )
    height = small.shape[0]
    half = hidden * hidden // 2

    def step(kernel, name, args, rows):
        kept, out, *sends = call(
            kernel,
            name,
            args,
            [((height, pairs), bf16), ((rows, pairs), f32)] + [((height + rows, pairs), bf16)] * 3,
            [],
            10**6,
        )
        return kept, out, sends

    out_came = swap(out_part[half:].astype(bf16), 1)
    kept, out, sends = step(
        join_kernel, "join", (small, swap(small, 1), out_part, out_came), half // yxs
    )
    came = {k: swap(sends[k - 1], k * 2) for k in (3, 1, 2)}
    kept, delta, grad = lax.optimization_barrier((kept, delta, grad))
    kept, out, sends = step(merge_kernel, "merge", (kept, out, came[1], came[2], came[3]), half // yxs // zs)
    came = {k: swap(sends[k - 1], k * 2 * yxs) for k in (3, 2, 1)}
    gain_out, left_out, right_out, out_share, bias_out = call(
        functools.partial(finish_kernel, 1.0 / columns),
        "finish",
        (kept, out, came[1], came[2], came[3]),
        [
            ((1, channels), f32),
            ((hidden, channels), f32),
            ((hidden, channels), f32),
            ((hidden * hidden // count, pairs), f32),
            ((1, pairs), f32),
        ],
        [((2 * hidden + 16, channels), f32), ((hidden * hidden // count, pairs), f32)],
        10**6,
        remote_out=True,
    )
    return (
        delta,
        grad,
        gain_out.reshape(channels),
        left_out.T,
        right_out.T,
        out_share,
        bias_out.reshape(pairs),
    )


def solution(mesh):
    in_specs = (P(None, ("col", "row"), None), P(), P(), P(), P(), P(), P("row", "col", None))
    out_specs = (
        P("row", "col", None),
        P(None, ("col", "row"), None),
        P(),
        P(),
        P(),
        P(("row", "col"), None),
        P(),
    )
    one_row = mesh.shape["row"] == 32 and mesh.shape["col"] == 1
    body = on_device_row if one_row else on_device
    return jax.shard_map(
        body, mesh=mesh, in_specs=in_specs, out_specs=out_specs, check_vma=False
    )
```

```python
import functools
import math

import jax
import jax.numpy as jnp
from jax import lax
from jax.experimental import pallas as pl
from jax.experimental.pallas import tpu as pltpu
from jax.sharding import PartitionSpec as P

ln_epsilon = 1e-05


def from_root(value, axis, root):
    mine = lax.axis_index(axis) == root
    return lax.psum(jnp.where(mine, value, jnp.zeros_like(value)), axis)


def layer_norm_output(homolog_features, standardize_multiplier):
    value_entries = homolog_features.astype(jnp.float32)
    centred = value_entries - jnp.mean(value_entries, axis=-1, keepdims=True)
    reciprocal_deviation = lax.rsqrt(
        jnp.mean(centred * centred, axis=-1, keepdims=True) + ln_epsilon
    )
    scaled_rows = centred * reciprocal_deviation
    normalized_rows = (scaled_rows * standardize_multiplier).astype(jnp.bfloat16)
    return (scaled_rows, reciprocal_deviation, normalized_rows)


def on_device(
    homolog_features,
    standardize_multiplier,
    first_factor_weights,
    second_factor_weights,
    output_projection_matrix,
    output_bias,
    pair_cotangent,
):
    sequence_count, local_residues, channel_count = homolog_features.shape
    hidden = first_factor_weights.shape[1]
    pair_channels = output_projection_matrix.shape[1]
    row_count = lax.axis_size("row")
    col_count = lax.axis_size("col")
    ratio = row_count // col_count
    row_index = lax.axis_index("row")
    col_index = lax.axis_index("col")
    scaled_rows, reciprocal_deviation, normalized_rows = layer_norm_output(
        homolog_features, standardize_multiplier
    )
    left_own = jnp.dot(
        normalized_rows, first_factor_weights, preferred_element_type=jnp.float32
    ).astype(jnp.bfloat16)
    right_own = jnp.dot(
        normalized_rows, second_factor_weights, preferred_element_type=jnp.float32
    ).astype(jnp.bfloat16)
    left_cols, right_cols = (
        lax.all_gather(
            left_own.reshape(sequence_count, local_residues * hidden), "row", axis=1, tiled=True
        ),
        lax.all_gather(
            right_own.reshape(sequence_count, local_residues * hidden), "row", axis=1, tiled=True
        ),
    )
    col_res = local_residues * row_count
    row_res = col_res // ratio
    offset = row_index % ratio * row_res
    piece_flat = lax.dynamic_slice_in_dim(left_cols, offset * hidden, row_res * hidden, 1)
    left_rows = from_root(piece_flat, "col", row_index // ratio).reshape(
        sequence_count, row_res, hidden
    )
    right_block = right_cols.reshape(sequence_count, col_res, hidden)
    group = math.gcd(row_res, max(1, 512 // col_res))
    blocks = row_res // group
    left_steps = jnp.transpose(
        left_rows.reshape(sequence_count, blocks, group, hidden), (1, 0, 2, 3)
    )
    grad_steps = pair_cotangent.reshape(blocks, group, col_res, pair_channels)
    per_homolog_weight = 1.0 / sequence_count

    def pair_step(carried, inputs):
        out_acc, right_acc = carried
        left_blk, grad_blk = inputs
        outer = (
            jnp.einsum("sic,sjd->ijcd", left_blk, right_block, preferred_element_type=jnp.float32)
            * per_homolog_weight
        )
        outer_bf = outer.reshape(group * col_res, hidden * hidden).astype(jnp.bfloat16)
        update = (
            jnp.dot(outer_bf, output_projection_matrix, preferred_element_type=jnp.float32)
            + output_bias
        ).astype(jnp.bfloat16)
        grad_rows = grad_blk.reshape(group * col_res, pair_channels)
        out_acc = out_acc + lax.dot_general(
            outer_bf, grad_rows, (((0,), (0,)), ((), ())), preferred_element_type=jnp.float32
        )
        outer_grad = jnp.dot(
            grad_rows, output_projection_matrix.T, preferred_element_type=jnp.float32
        ).astype(jnp.bfloat16)
        outer_grad = outer_grad.reshape(group, col_res, hidden, hidden)
        left_blk_grad = (
            jnp.einsum("ijcd,sjd->sic", outer_grad, right_block, preferred_element_type=jnp.float32)
            * per_homolog_weight
        )
        right_acc = (
            right_acc
            + jnp.einsum("ijcd,sic->sjd", outer_grad, left_blk, preferred_element_type=jnp.float32)
            * per_homolog_weight
        )
        return (
            (out_acc, right_acc),
            (update.reshape(group, col_res, pair_channels), left_blk_grad),
        )

    initial_carry = (
        jnp.zeros((hidden * hidden, pair_channels), jnp.float32),
        jnp.zeros((sequence_count, col_res, hidden), jnp.float32),
    )
    (out_acc, right_part), (updates, first_factor_pieces) = lax.scan(
        pair_step, initial_carry, (left_steps, grad_steps)
    )
    pair_delta = updates.reshape(row_res, col_res, pair_channels)
    left_part = jnp.transpose(first_factor_pieces, (1, 0, 2, 3)).reshape(
        sequence_count, row_res * hidden
    )
    right_flat = right_part.reshape(sequence_count, col_res * hidden)
    left_row = lax.psum(left_part, "col")
    owner = row_index // ratio == col_index
    slotted = lax.dynamic_update_slice_in_dim(
        jnp.zeros((sequence_count, col_res * hidden), jnp.float32),
        jnp.where(owner, left_row, 0.0),
        offset * hidden,
        1,
    )
    first_factor_total, right_sum = (
        lax.psum_scatter(slotted, "row", scatter_dimension=1, tiled=True),
        lax.psum_scatter(right_flat, "row", scatter_dimension=1, tiled=True),
    )
    left_bf = first_factor_total.reshape(sequence_count, local_residues, hidden).astype(
        jnp.bfloat16
    )
    right_bf = right_sum.reshape(sequence_count, local_residues, hidden).astype(jnp.bfloat16)
    normed_grad = jnp.dot(
        left_bf, first_factor_weights.T, preferred_element_type=jnp.float32
    ) + jnp.dot(right_bf, second_factor_weights.T, preferred_element_type=jnp.float32)
    scaled_gradient = normed_grad * standardize_multiplier
    centering_term = jnp.mean(scaled_gradient, axis=-1, keepdims=True)
    gradient_slope_term = jnp.mean(scaled_gradient * scaled_rows, axis=-1, keepdims=True)
    alignment_gradient = (
        reciprocal_deviation
        * (scaled_gradient - centering_term - scaled_rows * gradient_slope_term)
    ).astype(jnp.bfloat16)
    gain_part = jnp.sum(normed_grad * scaled_rows, axis=(0, 1))
    left_weight = jnp.einsum(
        "srm,srh->mh", normalized_rows, left_bf, preferred_element_type=jnp.float32
    )
    right_weight = jnp.einsum(
        "srm,srh->mh", normalized_rows, right_bf, preferred_element_type=jnp.float32
    )
    bias_part = jnp.sum(pair_cotangent, axis=(0, 1), dtype=jnp.float32)
    left_total, right_total, gain_total, bias_total = lax.psum(
        (left_weight, right_weight, gain_part, bias_part), ("row", "col")
    )
    out_share = lax.psum_scatter(out_acc, ("row", "col"), scatter_dimension=0, tiled=True)
    scale = 1.0 / (local_residues * row_count * col_count)
    return (
        pair_delta,
        alignment_gradient,
        gain_total * scale,
        left_total * scale,
        right_total * scale,
        out_share * scale,
        bias_total * scale,
    )


f32 = jnp.float32
bf16 = jnp.bfloat16


def mm(a, b):
    return lax.dot_general(a, b, (((1,), (0,)), ((), ())), preferred_element_type=f32)


def mm_t(a, b):
    return lax.dot_general(a, b, (((1,), (1,)), ((), ())), preferred_element_type=f32)


def fetch(pairs, sems):
    copies = [pltpu.make_async_copy(a, b, sems.at[n]) for n, (a, b) in enumerate(pairs)]
    for copy in copies:
        copy.start()
    return copies


def normalise(x):
    centred = x - jnp.mean(x, axis=-1, keepdims=True)
    recip = lax.rsqrt(jnp.mean(centred * centred, axis=-1, keepdims=True) + ln_epsilon)
    return centred * recip, recip


def factor_kernel(
    x_hbm, gain_hbm, w1_hbm, w2_hbm, cot_hbm,
    send0_ref, send1_ref, send2_ref, send3_ref,
    x_ref, gain_ref, w1_ref, w2_ref, cot_ref, rows, twin, cots, moved, sems,
):
    copies = fetch(
        [(x_hbm, x_ref), (gain_hbm, gain_ref), (w1_hbm, w1_ref), (w2_hbm, w2_ref), (cot_hbm, cot_ref)],
        sems,
    )
    sends = (send0_ref, send1_ref, send2_ref, send3_ref)
    seqs, res, _ = x_ref.shape
    hidden = w1_ref.shape[0]
    columns = cot_ref.shape[1]
    devices = columns // res
    copies[0].wait()
    rows[...] = x_ref[...].astype(f32)
    for copy in copies[1:]:
        copy.wait()
    both = jnp.concatenate([w1_ref[...], w2_ref[...]], axis=0)
    low = lax.broadcasted_iota(jnp.int32, (hidden, 2 * seqs), 1) < seqs
    for r in range(res):
        scaled, _ = normalise(rows[:, r, :])
        normed = (scaled * gain_ref[...]).astype(bf16)
        twin[r] = mm_t(both, jnp.concatenate([normed, normed], axis=0))
        even = twin[r, pl.ds(0, hidden, stride=2), :]
        odd = twin[r, pl.ds(1, hidden, stride=2), :]
        piece = jnp.where(low, even, odd).astype(bf16)
        for send_ref in sends:
            send_ref[r * hidden : (r + 1) * hidden, :] = piece
    for r in range(res):
        cots[r * columns : (r + 1) * columns, :] = cot_ref[r].astype(f32)
    for r in range(res):
        for q in range(res):
            block = cots[pl.ds(r * columns + q, devices, stride=res), :]
            at = (r * res + q) * (devices + 1)
            moved[at : at + devices, :] = block
    index = lax.axis_index("row")
    per = res * res
    plane = devices // len(sends)
    for n in range(devices):
        block = moved[pl.ds(lax.bitwise_xor(index, n), per, stride=devices + 1), :]
        to = res * hidden + n % plane * per
        sends[n // plane][to : to + per, :] = block.astype(bf16)


def copy_kernel(*refs):
    for a, b in zip(refs[: len(refs) // 2], refs[len(refs) // 2 :]):
        b[...] = a[...]


def own_kernel(
    send_in, x_ref, gain_ref, w1_ref,
    send_ref, scaled_ref, normed_ref, recip_ref, diag_ref,
    rows,
):
    send_ref[...] = send_in[...]
    seqs, res, _ = x_ref.shape
    hidden = w1_ref.shape[0]
    rows[...] = x_ref[...].astype(f32)
    low = lax.broadcasted_iota(jnp.int32, (hidden, 2 * seqs), 1) < seqs
    for r in range(res):
        scaled, recip = normalise(rows[:, r, :])
        at = slice(r * seqs, (r + 1) * seqs)
        scaled_ref[at, :] = scaled
        recip_ref[at, :] = jnp.broadcast_to(recip, (seqs, recip_ref.shape[1]))
        normed = (scaled * gain_ref[...]).astype(bf16)
        normed_ref[at, :] = normed
        left = mm_t(w1_ref[...], jnp.concatenate([normed, normed], axis=0))
        zero = jnp.zeros_like(left)
        lanes = slice(r * 2 * seqs, (r + 1) * 2 * seqs)
        diag_ref[:hidden, lanes] = jnp.where(low, left, zero).astype(bf16)
        diag_ref[hidden:, lanes] = jnp.where(low, zero, left).astype(bf16)


def pack_kernel(height, *refs):
    held, sent = refs[: len(refs) // 2], refs[len(refs) // 2 :]
    cut = (held[0].shape[0] - height) // len(sent)
    for z, h in enumerate(held):
        factors = h[:height, :]
        for yx, s in enumerate(sent):
            s[z * height : (z + 1) * height, :] = factors
            to = len(held) * height + z * cut
            s[to : to + cut, :] = h[height + yx * cut : height + (yx + 1) * cut, :]


def prepare_kernel(
    out_w_ref, cot_ref, w1_in, w2_in,
    cot_t_ref, twin_left_ref, twin_right_ref, bias_ref, w1_ref, w2_ref,
    wide,
):
    hidden = twin_left_ref.shape[0] // 2
    res, columns, pairs = cot_ref.shape
    copy_kernel(w1_in, w2_in, w1_ref, w2_ref)
    wide[...] = out_w_ref[...].astype(f32)
    for d in range(hidden):
        at = (d % 2) * hidden
        twin_left_ref[at : at + hidden, (d // 2) * pairs : (d // 2 + 1) * pairs] = wide[
            pl.ds(d, hidden, stride=hidden), :
        ].astype(bf16)
    for q in range(hidden // 2):
        twin_right_ref[:, q * pairs : (q + 1) * pairs] = out_w_ref[
            q * 2 * hidden : (q + 1) * 2 * hidden, :
        ]
    total = jnp.zeros((1, pairs), f32)
    for r in range(res):
        cot = cot_ref[r].astype(f32)
        total = total + jnp.sum(cot, axis=0, keepdims=True)
        cot_t_ref[r * pairs : (r + 1) * pairs, :] = cot.T.astype(bf16)
    bias_ref[...] = jnp.broadcast_to(total, bias_ref.shape)


def sums_kernel(
    yxs, cot_t_ref, twin_left_ref, twin_right_ref, normed_ref, scaled_ref,
    w1_ref, w2_ref, bias_ref, diag_ref, *refs,
):
    mine, other = refs[:yxs], refs[yxs : 2 * yxs]
    small_ref, rights_ref, out_ref, grad_ref, spread_ref, wide, lefts, turned, cots, got_t, outs = refs[2 * yxs :]
    columns = rights_ref.shape[0]
    lanes = mine[0].shape[1]
    seqs = lanes // 2
    channels = normed_ref.shape[1]
    hidden = w1_ref.shape[0]
    twins = hidden // 2
    pairs = bias_ref.shape[1]
    res = cot_t_ref.shape[0] // pairs
    index = lax.axis_index("row")
    height = res * hidden
    per = res * res
    zs = columns // (2 * yxs * res)
    for yx in range(yxs):
        for z in range(zs):
            factors = slice(z * height, (z + 1) * height)
            first = zs * height + z * 2 * per
            for core, ref in enumerate((mine[yx], other[yx])):
                device = lax.bitwise_xor(index, z * 2 * yxs + yx * 2 + core)
                block = ref[factors, :].astype(f32)
                for r in range(res):
                    wide[pl.ds(device * res + r, hidden, stride=columns + 1), :] = block[
                        r * hidden : (r + 1) * hidden
                    ]
                block = ref[first + core * per : first + (core + 1) * per, :]
                at = pl.multiple_of(device * per, per)
                cots[pl.ds(at, per), :] = block.astype(f32)
    for r in range(res):
        got_t[r * pairs : (r + 1) * pairs, :] = cots[pl.ds(r, columns, stride=res), :].T.astype(bf16)
    for q in range(twins):
        here = slice(q * lanes, (q + 1) * lanes)
        at = q * (columns + 1)
        lefts[:, here] = wide[at : at + columns, :].astype(bf16)
        at = (twins + q) * (columns + 1)
        rights_ref[:, here] = wide[at : at + columns, :].astype(bf16)

    def summed(cots, factors, weights, out):
        for q in range(0, twins, 2):
            block = mm(cots[...], factors[:, q * lanes : (q + 2) * lanes]).astype(bf16)
            for r in range(res):
                for e in range(2):
                    out[(q + e) * pairs : (q + e + 1) * pairs, r * lanes : (r + 1) * lanes] = block[
                        r * pairs : (r + 1) * pairs, e * lanes : (e + 1) * lanes
                    ]
        t = mm(weights[...], out[...]).T
        parts = [
            t[r * lanes : r * lanes + seqs, :hidden] + t[r * lanes + seqs : (r + 1) * lanes, hidden:]
            for r in range(res)
        ]
        return jnp.concatenate(parts, axis=0) * (1.0 / seqs)

    left_sum = summed(cot_t_ref, rights_ref, twin_left_ref, spread_ref)
    share_kernel(res, diag_ref, spread_ref, out_ref, outs)
    right_sum = summed(got_t, lefts, twin_right_ref, turned)
    normed_grad = mm(left_sum.astype(bf16), w1_ref[...]) + mm(right_sum.astype(bf16), w2_ref[...])
    grad_ref[...] = normed_grad
    factors_t = jnp.concatenate([left_sum, right_sum], axis=1).T.astype(bf16)
    weights = mm(factors_t, normed_ref[...])
    gain_part = jnp.sum(normed_grad * scaled_ref[...], axis=0, keepdims=True)
    line = lax.broadcasted_iota(jnp.int32, (8, pairs), 0)
    parts = channels // pairs
    rows = small_ref.shape[0] // parts
    for n in range(parts):
        here = slice(n * pairs, (n + 1) * pairs)
        small_ref[n * rows : n * rows + 2 * hidden, :] = weights[:, here]
        small_ref[n * rows + 2 * hidden : (n + 1) * rows, :] = jnp.where(
            line == 0,
            gain_part[:, here],
            jnp.where(line == 1, bias_ref[:1, :], jnp.zeros((8, pairs), f32)),
        )


def share_kernel(res, diag_ref, spread_ref, out_ref, outs):
    hidden = diag_ref.shape[0] // 2
    pairs = out_ref.shape[1]
    seqs = diag_ref.shape[1] // (2 * res)
    grad = mm_t(diag_ref[...], spread_ref[...]) * (1.0 / seqs)
    for d in range(hidden):
        at = (d % 2) * hidden
        outs[d * (hidden + 1) : d * (hidden + 1) + hidden, :] = grad[
            at : at + hidden, (d // 2) * pairs : (d // 2 + 1) * pairs
        ]
    index = lax.axis_index("row")
    for place in range(hidden):
        chunk = lax.bitwise_xor(index, place % 4 * 8 + place // 4 % 4 * 2 + place // 16)
        out_ref[place * hidden : (place + 1) * hidden, :] = outs[
            pl.ds(chunk, hidden, stride=hidden + 1), :
        ]


def result_kernel(
    rights_ref, twin_left_ref, w1_ref, normed_ref, bias_ref, normed_grad_ref, scaled_ref, recip_ref, gain_ref,
    delta_ref, grad_ref,
    rows, mixed,
):
    res, _, pairs = delta_ref.shape
    seqs = grad_ref.shape[0]
    hidden = w1_ref.shape[0]
    left = mm_t(normed_ref[...], w1_ref[...]).astype(bf16)
    for d in range(hidden):
        at = (d % 2) * hidden
        part = mm(left, twin_left_ref[at : at + hidden, (d // 2) * pairs : (d // 2 + 1) * pairs])
        part = part.astype(bf16)
        for r in range(res):
            mixed[d * seqs : (d + 1) * seqs, r * pairs : (r + 1) * pairs] = part[
                r * seqs : (r + 1) * seqs, :
            ]
    delta = mm(rights_ref[...], mixed[...]) * (1.0 / seqs)
    for r in range(res):
        delta_ref[r] = (delta[:, r * pairs : (r + 1) * pairs] + bias_ref[...]).astype(bf16)
    scaled = scaled_ref[...]
    scaled_grad = normed_grad_ref[...] * gain_ref[...]
    centre = jnp.mean(scaled_grad, axis=-1, keepdims=True)
    slope = jnp.mean(scaled_grad * scaled, axis=-1, keepdims=True)
    grad = recip_ref[:, :1] * (scaled_grad - centre - scaled * slope)
    for r in range(res):
        rows[:, r, :] = grad[r * seqs : (r + 1) * seqs, :]
    grad_ref[...] = rows[...].astype(bf16)


def split(small, out, small_ref, out_ref, sends):
    small = small.astype(bf16)
    rows = out_ref.shape[0]
    small_ref[...] = small
    out_ref[...] = out[:rows]
    for k, send in enumerate(sends):
        send[: small.shape[0], :] = small
        send[small.shape[0] :, :] = out[(k + 1) * rows : (k + 2) * rows].astype(bf16)


def total(small_ref, out_ref, came):
    height = small_ref.shape[0]
    one, two, three = (c[:height, :].astype(f32) for c in came)
    small = (small_ref[...].astype(f32) + one) + (two + three)
    one, two, three = (c[height:, :].astype(f32) for c in came)
    return small, (out_ref[...] + one) + (two + three)


def join_kernel(small_in, small_came, out_in, out_came, small_ref, out_ref, *sends):
    kept = out_in[: out_came.shape[0], :] + out_came[...].astype(f32)
    split(small_in[...] + small_came[...], kept, small_ref, out_ref, sends)


def merge_kernel(small_in, out_in, one, two, three, small_ref, out_ref, *sends):
    small, out = total(small_in, out_in, (one, two, three))
    split(small, out, small_ref, out_ref, sends)


def finish_kernel(
    scale, small_in, out_in, one, two, three,
    gain_hbm, left_hbm, right_hbm, out_hbm, bias_hbm,
    whole, out_ref, sems,
):
    hidden = left_hbm.shape[0]
    pairs = bias_hbm.shape[1]
    small, out = total(small_in, out_in, (one, two, three))
    rows = whole.shape[0]
    for n in range(whole.shape[1] // pairs):
        whole[:, n * pairs : (n + 1) * pairs] = small[n * rows : (n + 1) * rows] * scale
    out_ref[...] = out * scale
    copies = fetch(
        [
            (whole.at[2 * hidden : 2 * hidden + 1, :], gain_hbm),
            (whole.at[:hidden, :], left_hbm),
            (whole.at[hidden : 2 * hidden, :], right_hbm),
            (out_ref, out_hbm),
            (whole.at[2 * hidden + 1 : 2 * hidden + 2, :pairs], bias_hbm),
        ],
        sems,
    )
    for copy in copies:
        copy.wait()


def call(kernel, name, args, outs, scratch, flops, remote_in=False, remote_out=False, vmem=16):
    moved = sum(a.size * a.dtype.itemsize for a in args)
    space = lambda far: pl.BlockSpec(memory_space=pltpu.HBM if far else pltpu.VMEM)
    sems = max(len(args) * remote_in, len(outs) * remote_out)
    shapes = [pltpu.VMEM(s, d) for s, d in scratch]
    if sems:
        shapes.append(pltpu.SemaphoreType.DMA((sems,)))
    return pl.pallas_call(
        kernel,
        out_shape=[jax.ShapeDtypeStruct(s, d) for s, d in outs],
        in_specs=[space(remote_in)] * len(args),
        out_specs=[space(remote_out)] * len(outs),
        scratch_shapes=shapes,
        compiler_params=pltpu.CompilerParams(vmem_limit_bytes=vmem * 1024 * 1024),
        cost_estimate=pl.CostEstimate(flops=flops, bytes_accessed=moved, transcendentals=0),
        name=name,
    )(*args)


def swap(value, step):
    count = lax.axis_size("row")
    return lax.ppermute(value, "row", [(i, i ^ step) for i in range(count)])


def on_device_row(
    homolog_features,
    standardize_multiplier,
    first_factor_weights,
    second_factor_weights,
    output_projection_matrix,
    output_bias,
    pair_cotangent,
):
    seqs, res, channels = homolog_features.shape
    hidden = first_factor_weights.shape[1]
    pairs = output_projection_matrix.shape[1]
    count = lax.axis_size("row")
    columns = res * count
    own = seqs * res
    lanes = 2 * seqs
    twins = hidden // 2
    gain = standardize_multiplier.reshape(1, channels)
    bias = output_bias.reshape(1, pairs)
    w1, w2 = first_factor_weights.T, second_factor_weights.T
    wide = (2 * hidden, twins * pairs)

    zs, yxs = 4, 4
    height = res * hidden
    sends = call(
        factor_kernel,
        "factors",
        (homolog_features, gain, w1, w2, pair_cotangent),
        [
            *[((height + res * columns // zs, lanes), bf16)] * zs,
        ],
        [
            ((seqs, res, channels), bf16),
            ((1, channels), f32),
            ((hidden, channels), bf16),
            ((hidden, channels), bf16),
            ((res, columns, pairs), bf16),
            ((seqs, res, channels), f32),
            ((res, 2 * hidden, lanes), f32),
            ((res * columns, pairs), f32),
            ((res * res * (count + 1), pairs), f32),
        ],
        10**6,
        remote_in=True,
        vmem=60,
    )
    swapped = {z: swap(sends[z], z * 2 * yxs) for z in (3, 2, 1)}
    own_send, scaled, normed, recip, diag = call(
        own_kernel,
        "own",
        (sends[0], homolog_features, gain, w1),
        [
            (sends[0].shape, bf16),
            ((own, channels), f32),
            ((own, channels), bf16),
            ((own, 128), f32),
            ((2 * hidden, res * lanes), bf16),
        ],
        [((seqs, res, channels), f32)],
        10**6,
    )
    sent = call(
        functools.partial(pack_kernel, height),
        "pack",
        [own_send] + [swapped[z] for z in range(1, zs)],
        [((zs * height + zs * 2 * res * res, lanes), bf16)] * yxs,
        [],
        10**6,
    )
    mine = [sent[0]] + [swap(sent[yx], yx * 2) for yx in range(1, yxs)]
    prepared = call(
        prepare_kernel,
        "prepare",
        (output_projection_matrix, pair_cotangent, w1, w2),
        [
            ((res * pairs, columns), bf16),
            (wide, bf16),
            (wide, bf16),
            ((8, pairs), f32),
            (w1.shape, bf16),
            (w2.shape, bf16),
        ],
        [((hidden * hidden, pairs), f32)],
        10**6,
    )
    mine[0], prepared = lax.optimization_barrier((mine[0], prepared))
    cot_t, twin_left, twin_right, bias_part, w1, w2 = prepared
    other = [swap(m, 1) for m in mine]
    small, rights, out_part, normed_grad = call(
        functools.partial(sums_kernel, yxs),
        "sums",
        (
            cot_t, twin_left, twin_right, normed, scaled, w1, w2, bias_part, diag, *mine, *other,
        ),
        [
            ((channels // pairs * (2 * hidden + 8), pairs), f32),
            ((columns, hidden * seqs), bf16),
            ((hidden * hidden, pairs), f32),
            ((own, channels), f32),
        ],
        [
            ((twins * pairs, res * lanes), bf16),
            (((columns + 1) * hidden, lanes), f32),
            ((columns, hidden * seqs), bf16),
            ((twins * pairs, res * lanes), bf16),
            ((res * columns, pairs), f32),
            ((res * pairs, columns), bf16),
            ((hidden * (hidden + 1), pairs), f32),
        ],
        10**6,
    )
    delta, grad = call(
        result_kernel,
        "results",
        (rights, twin_left, w1, normed, bias, normed_grad, scaled, recip, gain),
        [((res, columns, pairs), bf16), ((seqs, res, channels), bf16)],
        [((seqs, res, channels), f32), ((hidden * seqs, res * pairs), bf16)],
        10**6,
    )
    height = small.shape[0]
    half = hidden * hidden // 2

    def step(kernel, name, args, rows):
        kept, out, *sends = call(
            kernel,
            name,
            args,
            [((height, pairs), bf16), ((rows, pairs), f32)] + [((height + rows, pairs), bf16)] * 3,
            [],
            10**6,
        )
        return kept, out, sends

    out_came = swap(out_part[half:].astype(bf16), 1)
    kept, out, sends = step(
        join_kernel, "join", (small, swap(small, 1), out_part, out_came), half // yxs
    )
    came = {k: swap(sends[k - 1], k * 2) for k in (3, 1, 2)}
    kept, delta, grad = lax.optimization_barrier((kept, delta, grad))
    kept, out, sends = step(merge_kernel, "merge", (kept, out, came[1], came[2], came[3]), half // yxs // zs)
    came = {k: swap(sends[k - 1], k * 2 * yxs) for k in (3, 2, 1)}
    gain_out, left_out, right_out, out_share, bias_out = call(
        functools.partial(finish_kernel, 1.0 / columns),
        "finish",
        (kept, out, came[1], came[2], came[3]),
        [
            ((1, channels), f32),
            ((hidden, channels), f32),
            ((hidden, channels), f32),
            ((hidden * hidden // count, pairs), f32),
            ((1, pairs), f32),
        ],
        [((2 * hidden + 8, channels), f32), ((hidden * hidden // count, pairs), f32)],
        10**6,
        remote_out=True,
    )
    return (
        delta,
        grad,
        gain_out.reshape(channels),
        left_out.T,
        right_out.T,
        out_share,
        bias_out.reshape(pairs),
    )


def solution(mesh):
    in_specs = (P(None, ("col", "row"), None), P(), P(), P(), P(), P(), P("row", "col", None))
    out_specs = (
        P("row", "col", None),
        P(None, ("col", "row"), None),
        P(),
        P(),
        P(),
        P(("row", "col"), None),
        P(),
    )
    one_row = mesh.shape["row"] == 32 and mesh.shape["col"] == 1
    body = on_device_row if one_row else on_device
    return jax.shard_map(
        body, mesh=mesh, in_specs=in_specs, out_specs=out_specs, check_vma=False
    )
```
